256 devices in a mesh: section: 8 (over x, core), dp: 32 (over z, y).
Axes of the slice: x: 4, y: 4, z: 8, core: 2. Of those that a mesh axis runs over, the one named last changes fastest.
Arguments:
- saved_inputs: bfloat16 [8, 32, 4, 32, 4096], P('section', 'dp'), may hold values from -6 to 6
- saved_queries: bfloat16 [8, 32, 4, 32, 4096], P('section', 'dp'), may hold values from -6 to 6
- norm_gain: float32 [8, 4096], P('section'), may hold values from 0.1 to 1.9
- key_weight: bfloat16 [8, 4096, 512], P('section'), may hold values from -0.09375 to 0.09375
- value_weight: bfloat16 [8, 4096, 512], P('section'), may hold values from -0.09375 to 0.09375
- out_cotangent: bfloat16 [32, 4, 32, 4096], P('dp'), may hold values from -6 to 6
- token_counts: int32 [32, 4], P('dp'), may hold values from 8 to 32
- segment_ids: int32 [32, 4, 32], P('dp'), may hold values from 0 to 3, never falling along the last dimension, each value on 1 to 16 neighbouring positions
Outputs:
- input_grads: bfloat16 [8, 32, 4, 32, 4096], P('section', 'dp')
- key_weight_grad: float32 [8, 4096, 512], P('section', 'dp')
- value_weight_grad: float32 [8, 4096, 512], P('section', 'dp')
- gain_grad: float32 [8, 4096], P('section')
The draws below stay inside these ranges and needn't reach their ends.
Inputs may be any that keep to these rules, and one draw needn't show every extreme that they name: `segment_ids`: within each micro-batch the segment ids never fall.
All inputs are finite; a program needn't handle non-finite values.
Results may differ from the reference program's by a relative error of at most 0.034.
Values may be sent and summed in bfloat16 or wider, within the bound.
A program may use at most 128 MiB of HBM per device.

```python
import math
import jax
import jax.numpy as jnp
import numpy as np
from jax import lax

HD = 128
HEADS = 32
KVH = 4
D = 4096
KVW = 512
M = 4
ROWS = 32
N_SECTION = 8
N_DP = 32


def with_ends(values, stream_key, least, largest):
    extent = values.shape
    index_at = [jax.random.randint(jax.random.fold_in(stream_key, axis), (), 0, extent[axis]) for axis in range(len(extent))]
    values = values.at[tuple(index_at)].set(least)
    longest = extent.index(max(extent))
    index_at[longest] = (index_at[longest] + 1) % extent[longest]
    return values.at[tuple(index_at)].set(largest)


def block_scale(own_key, extent, split, least, high):
    gain, own = 1.0, jax.random.fold_in(own_key, 6)
    for axis_at, shards_of in split:
        draws = jnp.exp(jax.random.uniform(jax.random.fold_in(own, axis_at), (shards_of,), jnp.float32, least / len(split), high / len(split)))
        gain = gain * jnp.repeat(draws, extent[axis_at] // shards_of).reshape([-1 if axis == axis_at else 1 for axis in range(len(extent))])
    return gain


def split_up(count, total, limit, skew):
    loads = [(1 << 20) // math.isqrt(grade ** skew) + 1 for grade in range(2, count + 1)]
    rest, holding = total - limit - (count - 1), [1] * (count - 1)
    while rest > 0:
        candidates = [i for i in range(count - 1) if holding[i] < limit]
        pool, remaining = sum([loads[i] for i in candidates]), rest
        for i in candidates:
            extra = min(limit - holding[i], max(1, remaining * loads[i] // pool), rest)
            holding[i] = holding[i] + extra
            rest = rest - extra
    return np.array([limit] + holding)


def ragged(rng, count, total, reach, slope):
    if count == 2:
        one = jax.random.randint(rng, (), max(1, total - reach), min(reach, total - 1) + 1)
        return jnp.stack([one, total - one])
    lengths = jnp.asarray(split_up(count, total, reach, slope), jnp.int32)
    pairs = (count - 1) // 2
    giver, taker = lengths[1:1 + 2 * pairs:2], lengths[2:2 + 2 * pairs:2]
    slack = jnp.minimum(giver - 1, reach - taker)
    passed = jax.random.randint(jax.random.fold_in(rng, 1), (pairs,), 0, 1 << 20) % (slack + 1)
    lengths = lengths.at[1:1 + 2 * pairs:2].set(giver - passed).at[2:2 + 2 * pairs:2].set(taker + passed)
    return lengths[jax.random.permutation(jax.random.fold_in(rng, 2), count)]


def scatter_about(stream_key, extent, spread, reach, cuts=(), held_as=jnp.bfloat16):
    level = block_scale(stream_key, extent, cuts, -0.22, 0.18) if cuts else 1.0
    result = jax.random.normal(stream_key, extent, jnp.float32) * spread * level
    return jnp.minimum(jnp.maximum(result, -reach), reach).astype(held_as)


def setup_inputs(seed: int = 0) -> dict:
    streams_of = jax.random.split(jax.random.key(seed), 9)
    saved_inputs = scatter_about(streams_of[0], (N_SECTION, N_DP, M, ROWS, D), 1.0, 6.0, ((0, 8), (1, 32)))
    saved_queries = scatter_about(streams_of[1], (N_SECTION, N_DP, M, ROWS, D), 1.0, 6.0, ((0, 8), (1, 32)))
    norm_gain = jnp.clip(1.0 + 0.18 * jax.random.normal(streams_of[2], (N_SECTION, D), jnp.float32), 0.1, 1.9)
    key_weight = scatter_about(streams_of[3], (N_SECTION, D, KVW), D ** -0.5, 0.09375, ((0, 8),))
    value_weight = scatter_about(streams_of[4], (N_SECTION, D, KVW), D ** -0.5, 0.09375, ((0, 8),))
    out_cotangent = scatter_about(streams_of[5], (N_DP, M, ROWS, D), 1.0, 6.0, ((0, 32),))
    token_counts = with_ends(jax.random.randint(streams_of[6], (N_DP, M), ROWS // 4, ROWS + 1), jax.random.fold_in(streams_of[6], 1), ROWS // 4, ROWS).astype(jnp.int32)
    segment_ids = jax.vmap(lambda own: jnp.searchsorted(jnp.cumsum(ragged(own, 4, ROWS, ROWS // 2, 1)), jnp.arange(ROWS), side="right"))(jax.random.split(streams_of[7], N_DP * M)).reshape((N_DP, M, ROWS)).astype(jnp.int32)
    return {"saved_inputs": saved_inputs, "saved_queries": saved_queries, "norm_gain": norm_gain, "key_weight": key_weight, "value_weight": value_weight, "out_cotangent": out_cotangent, "token_counts": token_counts, "segment_ids": segment_ids}


EPS = 1e-05

def normalize(features, gain_row):
    inverse = lax.rsqrt(lax.optimization_barrier(jnp.mean(features * features, axis=-1, keepdims=True)) + EPS)
    return features * inverse * gain_row

def to_low(values_f32):
    return lax.optimization_barrier(values_f32.astype(jnp.bfloat16)).astype(jnp.float32)

def layer_backward(inputs, queries, gain_row, key_weight, value_weight, out_grad, count, segments):
    row_count = inputs.shape[0]
    group_heads = HEADS // KVH
    normed_f32, norm_pull = jax.vjp(normalize, inputs.astype(jnp.float32), gain_row)
    normed = normed_f32.astype(jnp.bfloat16)
    keys = jnp.dot(normed, key_weight, preferred_element_type=jnp.float32).astype(jnp.bfloat16)
    values = jnp.dot(normed, value_weight, preferred_element_type=jnp.float32).astype(jnp.bfloat16)
    positions = jnp.arange(row_count, dtype=jnp.int32)
    is_valid = positions < count
    allowed = (positions[None, :] <= positions[:, None]) & (segments[None, :] == segments[:, None]) & is_valid[None, :] | (positions[None, :] == positions[:, None])
    query_heads = queries.reshape(row_count, KVH, group_heads, HD).astype(jnp.float32)
    key_heads = keys.reshape(row_count, KVH, HD).astype(jnp.float32)
    value_heads = values.reshape(row_count, KVH, HD).astype(jnp.float32)
    score_scale = HD ** (-0.5)
    scores = jnp.einsum('igad,jgd->gaij', query_heads, key_heads) * score_scale
    weights = jnp.where(allowed, jnp.exp(scores), 0.0)
    probabilities = weights / lax.optimization_barrier(jnp.sum(weights, axis=-1, keepdims=True))
    probs_low = to_low(probabilities)
    head_grad = jnp.where(is_valid[:, None], out_grad, jnp.zeros_like(out_grad))
    head_grad = head_grad.reshape(row_count, KVH, group_heads, HD).astype(jnp.float32)
    value_grad = jnp.einsum('gaij,igad->jgd', probs_low, head_grad).astype(jnp.bfloat16).reshape(row_count, KVW)
    prob_grad = jnp.einsum('igad,jgd->gaij', head_grad, value_heads)
    score_grad = probabilities * (prob_grad - lax.optimization_barrier(jnp.sum(probabilities * prob_grad, axis=-1, keepdims=True))) * score_scale
    score_low = to_low(score_grad)
    key_grad = jnp.einsum('gaij,igad->jgd', score_low, query_heads).astype(jnp.bfloat16).reshape(row_count, KVW)
    normed_grad = jnp.dot(key_grad, key_weight.T, preferred_element_type=jnp.float32) + jnp.dot(value_grad, value_weight.T, preferred_element_type=jnp.float32)
    input_pull, gain_term = norm_pull(normed_grad)
    in_grad = (out_grad.astype(jnp.float32) + input_pull).astype(jnp.bfloat16)
    key_term = jnp.dot(normed.T, key_grad, preferred_element_type=jnp.float32)
    value_term = jnp.dot(normed.T, value_grad, preferred_element_type=jnp.float32)
    return (in_grad, key_term, value_term, gain_term)

def reference(saved_inputs, saved_queries, norm_gain, key_weight, value_weight, out_cotangent, token_counts, segment_ids):
    sections = saved_inputs.shape[0]
    pass_all = jax.vmap(layer_backward, in_axes=(0, 0, None, None, None, 0, 0, 0))
    upper_grad = out_cotangent
    input_list, key_list, value_list, gain_list = ([], [], [], [])
    for layer_id in reversed(range(sections)):
        gain_row = norm_gain[layer_id]
        key_mat = key_weight[layer_id]
        value_mat = value_weight[layer_id]

        def replica(state_carry, pieces):
            inputs, queries, grads_in, counts, segments = pieces
            in_grad, key_term, value_term, gain_term = pass_all(inputs, queries, gain_row, key_mat, value_mat, grads_in, counts, segments)
            both_terms = jnp.concatenate([lax.optimization_barrier(jnp.sum(key_term, axis=0)), lax.optimization_barrier(jnp.sum(value_term, axis=0))], axis=1)
            sent = to_low(both_terms)
            return ((state_carry[0] + sent, state_carry[1] + lax.optimization_barrier(jnp.sum(gain_term, axis=0))), in_grad)
        initial = (jnp.zeros((D, 2 * KVW), jnp.float32), jnp.zeros((D,), jnp.float32))
        (weight_total, gain_total), layer_grads = lax.scan(replica, initial, (saved_inputs[layer_id], saved_queries[layer_id], upper_grad, token_counts, segment_ids))
        upper_grad = layer_grads
        input_list.append(layer_grads)
        key_list.append(weight_total[:, :KVW])
        value_list.append(weight_total[:, KVW:])
        gain_list.append(gain_total)
    input_grads = jnp.stack(input_list[::-1])
    key_weight_grad = jnp.stack(key_list[::-1])
    value_weight_grad = jnp.stack(value_list[::-1])
    gain_grad = jnp.stack(gain_list[::-1])
    return (input_grads, key_weight_grad, value_weight_grad, gain_grad)
```

```python
import functools

import jax
import jax.numpy as jnp
from jax import lax
from jax.experimental import pallas as pl
from jax.experimental.pallas import tpu as pltpu
from jax.sharding import PartitionSpec as P

HD = 128
KVH = 4
EPS = 1e-05
NY = 4

f32 = jnp.float32
bf16 = jnp.bfloat16
MESH = pl.DeviceIdType.MESH


def dot(a, b):
    return jnp.dot(a, b, preferred_element_type=f32)


def dot_t(a, b):
    return lax.dot_general(a, b, (((1,), (1,)), ((), ())), preferred_element_type=f32)


def aligned(index, size):
    return pl.ds(pl.multiple_of(index * size, size), size)


def heads(rows, count):
    return jnp.concatenate([rows[:, a * HD : (a + 1) * HD] for a in range(count)], axis=0)


def normalise(x, gain, inv, normed):
    width = x.shape[1]

    def step(r, _):
        rows = aligned(r, 16)
        xb = x[rows, :].astype(f32)
        scale = lax.rsqrt(jnp.sum(xb * xb, axis=1, keepdims=True) * (1.0 / width) + EPS)
        inv[rows, :] = jnp.broadcast_to(scale, (16, 128))
        normed[rows, :] = (xb * scale * gain[...]).astype(bf16)
        return _

    lax.fori_loop(0, x.shape[0] // 16, step, 0)


def project(normed, weights, kv32, kvb):
    for p, w in enumerate(weights):
        cols = slice(p * w.shape[1], (p + 1) * w.shape[1])
        y = dot(normed[...], w[...])
        kv32[:, cols] = y
        kvb[:, cols] = y.astype(bf16)


def probabilities(m, q, kvb, seg, count, probs):
    n_rows, width = q.shape[1], q.shape[2]
    per_group = width // HD // KVH
    n = n_rows * per_group
    rows = aligned(m, n_rows)
    seg_i = jnp.broadcast_to(seg[pl.ds(m, 1), :], (n_rows, n))
    j = lax.broadcasted_iota(jnp.int32, (n_rows, n), 0)
    i = lax.rem(lax.broadcasted_iota(jnp.int32, (n_rows, n), 1), n_rows)
    seg_j = jnp.sum(jnp.where(i == j, seg_i, 0), axis=1, keepdims=True)
    allowed = ((j <= i) & (seg_i * per_group == seg_j) & (j < count)) | (i == j)
    for g in range(KVH):
        keys = kvb[rows, g * HD : (g + 1) * HD]
        queries = heads(q[m, :, g * per_group * HD : (g + 1) * per_group * HD], per_group)
        scores = dot_t(keys, queries) * (HD**-0.5)
        weights = jnp.where(allowed, jnp.exp(scores), 0.0)
        full = weights / jnp.sum(weights, axis=0, keepdims=True)
        probs[m, g] = jnp.where(i < count, full, 0.0)


def attend(m, gin, q, kvb, probs, both):
    n_rows, width = q.shape[1], q.shape[2]
    per_group = width // HD // KVH
    kv_cols = KVH * HD
    rows = aligned(m, n_rows)
    for g in range(KVH):
        values = kvb[rows, kv_cols + g * HD : kv_cols + (g + 1) * HD]
        head_grad = heads(gin[m, g], per_group)
        queries = heads(q[m, :, g * per_group * HD : (g + 1) * per_group * HD], per_group)
        p = probs[m, g]
        prob_grad = dot_t(values, head_grad)
        score_grad = p * (prob_grad - jnp.sum(p * prob_grad, axis=0, keepdims=True)) * (HD**-0.5)
        both[rows, kv_cols + g * HD : kv_cols + (g + 1) * HD] = dot(p.astype(bf16), head_grad).astype(bf16)
        both[rows, g * HD : (g + 1) * HD] = dot(score_grad.astype(bf16), queries).astype(bf16)


def kernel(
    ns, nz, x, q, gain, kw, vw, cot, seg, counts,
    gout, dk, dv, gg,
    inv, normed, normed_t, normed_all, kv32, kvb, probs, kwt, vwt,
    gin, gnext, grads, gacc, gain_y, gain_zs, gain_zr, ring_s, ring_r,
    cot_sem, next_s, next_r, out_sem, nt_s, nt_r, nt_l, kv_s, kv_r, gy_s, gy_r, gz_s, gz_r, ring_ss, ring_rs,
):
    micros, n_rows, width = q.shape
    total = micros * n_rows
    kv_cols = kw.shape[1]
    chunk = width // KVH
    feats = width // (nz * NY)
    sec = lax.axis_index("section")
    dp = lax.axis_index("dp")
    z, y = lax.div(dp, NY), lax.rem(dp, NY)
    is_last = sec == ns - 1
    is_first = sec == 0
    stages = nz.bit_length() - 1
    half = nz // 2

    def along_z(k):
        return lax.rem(z + k + nz, nz)

    def along_y(k):
        return lax.rem(y + k, NY)

    def flipped(b):
        return z + b - 2 * b * lax.rem(lax.div(z, b), 2)

    def device(zz, yy):
        return (sec, zz * NY + yy)

    y_peers = [device(z, along_y(k)) for k in range(1, NY)]
    up, down = device(along_z(1), y), device(along_z(-1), y)
    flips = [device(flipped(1 << i), y) for i in range(stages)]

    def remote(src, dst, ssem, rsem, dev):
        return pltpu.make_async_remote_copy(
            src_ref=src, dst_ref=dst, send_sem=ssem, recv_sem=rsem, device_id=dev, device_id_type=MESH
        )

    barrier = pltpu.get_barrier_semaphore()
    above, below = (lax.rem(sec + 1, ns), dp), (lax.rem(sec + ns - 1, ns), dp)
    greeted = y_peers + [up, down] + flips[1:] + [above, below]
    for peer in greeted:
        pl.semaphore_signal(barrier, inc=1, device_id=peer, device_id_type=MESH)

    def cot_copy(m, g):
        return pltpu.make_async_copy(
            cot.at[m, :, pl.ds(g * chunk, chunk)], gin.at[m, g], cot_sem.at[m, g]
        )

    @pl.when(is_last)
    def _():
        for m in range(micros):
            for g in range(KVH):
                cot_copy(m, g).start()

    normalise(x, gain, inv, normed)
    project(normed, (kw, vw), kv32, kvb)

    def each_probs(m, _):
        probabilities(m, q, kvb, seg, counts[m], probs)
        return _

    lax.fori_loop(0, micros, each_probs, 0)

    def turn(b, _):
        cols = aligned(b, 128)
        kwt[:, cols] = kw[cols, :].T
        vwt[:, cols] = vw[cols, :].T
        first = b * 128
        owner = lax.div(first, feats)
        at = lax.div(owner, NY) * feats + lax.rem(first, feats)
        normed_t[lax.rem(owner, NY), pl.ds(pl.multiple_of(at, 128), 128), :] = normed[:, cols].T
        return _

    lax.fori_loop(0, width // 128, turn, 0)
    gacc[...] = jnp.zeros_like(gacc)

    pl.semaphore_wait(barrier, len(greeted))

    def nt_copy(k):
        return remote(
            normed_t.at[along_y(k)], normed_all.at[:, pl.ds(k * total, total)], nt_s.at[k], nt_r.at[k], y_peers[k - 1]
        )

    for k in range(1, NY):
        nt_copy(k).start()
    own_nt = pltpu.make_async_copy(normed_t.at[y], normed_all.at[:, pl.ds(0, total)], nt_l)
    own_nt.start()

    def next_copy(m, g):
        return remote(gnext.at[m, g], gin.at[m, g], next_s.at[m, g], next_r.at[m, g], below)

    def out_copy(m, g):
        return pltpu.make_async_copy(
            gnext.at[m, g], gout.at[m, :, pl.ds(g * chunk, chunk)], out_sem.at[m, g]
        )

    def kv_copy(m, k):
        rows = aligned(m, n_rows)
        to = pl.ds(pl.multiple_of(k * total + m * n_rows, n_rows), n_rows)
        return remote(grads.at[rows, :], grads.at[to, :], kv_s.at[k, m], kv_r.at[k, m], y_peers[k - 1])

    def layer(m, carry):
        @pl.when(is_last)
        def _():
            for g in range(KVH):
                cot_copy(m, g).wait()

        @pl.when(jnp.logical_not(is_last))
        def _():
            for g in range(KVH):
                next_copy(m, g).wait_recv()

        attend(m, gin, q, kvb, probs, grads)
        rows = aligned(m, n_rows)
        both = grads[rows, :]
        scale = inv[rows, 0:1]
        pulled = jnp.sum(both.astype(f32) * kv32[rows, :], axis=1, keepdims=True) * (
            scale * scale * (1.0 / width)
        )
        for g in range(KVH):
            cols = slice(g * chunk, (g + 1) * chunk)
            grad = (dot(both[:, :kv_cols], kwt[:, cols]) + dot(both[:, kv_cols:], vwt[:, cols])) * scale
            xb = x[rows, cols].astype(f32)
            gnext[m, g] = (gin[m, g].astype(f32) + grad * gain[:, cols] - xb * pulled).astype(bf16)

            @pl.when(jnp.logical_not(is_first))
            def _():
                next_copy(m, g).start()

            out_copy(m, g).start()
            term = grad * xb
            gacc[:, cols] += term[0:8] + term[8:16] + term[16:24] + term[24:32]
        for k in range(1, NY):
            kv_copy(m, k).start()
        return carry

    lax.fori_loop(0, micros, layer, 0)

    part = width // 8
    gsum = jnp.sum(gacc[...], axis=0, keepdims=True)
    for r in range(8):
        gain_y[0, r : r + 1, :] = gsum[:, r * part : (r + 1) * part]

    def gy_copy(k):
        return remote(gain_y.at[0], gain_y.at[k], gy_s.at[k], gy_r.at[k], y_peers[k - 1])

    def gz_copy(i):
        return remote(gain_zs.at[i], gain_zr.at[i], gz_s.at[i], gz_r.at[i], flips[i])

    for k in range(1, NY):
        gy_copy(k).start()

    def gain_stage(i):
        if i == 0:
            for k in range(1, NY):
                gy_copy(k).wait_recv()
            summed = gain_y[0]
            for k in range(1, NY):
                summed = summed + gain_y[k]
        else:
            gz_copy(i - 1).wait_recv()
            summed = gain_zs[i - 1] + gain_zr[i - 1]
        if i < stages:
            gain_zs[i] = summed
            gz_copy(i).start()
        else:
            for r in range(8):
                gg[:, r * part : (r + 1) * part] = summed[r : r + 1, :]

    own_nt.wait()
    for k in range(1, NY):
        nt_copy(k).wait_recv()

    def kv_waits(m, _):
        for k in range(1, NY):
            kv_copy(m, k).wait_recv()
        return _

    lax.fori_loop(0, micros, kv_waits, 0)

    def piece(zz, h):
        return dot(normed_all[aligned(zz, feats), :], grads[:, h * kv_cols : (h + 1) * kv_cols])

    def ring_copy(way, t, h):
        return remote(
            ring_s.at[way, t, h], ring_r.at[way, t, h], ring_ss.at[way, t, h], ring_rs.at[way, t, h],
            (down, up)[way],
        )

    for t in range(half):
        sums = {}
        for way in range(2):
            target = along_z((t - half) if way == 0 else (half - t))
            for h in range(2):
                if t > 0 or h == way:
                    sums[way, h] = piece(target, h)
        for h in range(2):
            for way in range(2):
                if (way, h) in sums:
                    value = sums[way, h]
                    if t > 1 or (t == 1 and h == way):
                        ring_copy(way, t - 1, h).wait_recv()
                        value = value + ring_r[way, t - 1, h].astype(f32)
                    ring_s[way, t, h] = value.astype(bf16)
                    ring_copy(way, t, h).start()
        if t <= stages:
            gain_stage(t)
    for t in range(half, stages + 1):
        gain_stage(t)
    own = [piece(z, h) for h in range(2)]
    for h, out in enumerate((dk, dv)):
        value = own[h]
        for way in range(2):
            ring_copy(way, half - 1, h).wait_recv()
            value = value + ring_r[way, half - 1, h].astype(f32)
        out[...] = value

    def sent(m, carry):
        for g in range(KVH):
            @pl.when(jnp.logical_not(is_first))
            def _():
                next_copy(m, g).wait_send()

            out_copy(m, g).wait()
        for k in range(1, NY):
            kv_copy(m, k).wait_send()
        return carry

    lax.fori_loop(0, micros, sent, 0)
    for k in range(1, NY):
        nt_copy(k).wait_send()
        gy_copy(k).wait_send()
    for i in range(stages):
        gz_copy(i).wait_send()
    for t in range(half):
        for way in range(2):
            for h in range(2):
                if t > 0 or h == way:
                    ring_copy(way, t, h).wait_send()


def shards(ns, nd, saved_inputs, saved_queries, norm_gain, key_weight, value_weight, out_cotangent, token_counts, segment_ids):
    micros, n_rows, width = saved_inputs.shape[2:]
    kv_cols = key_weight.shape[2]
    total = micros * n_rows
    nz = nd // NY
    per_group = width // HD // KVH
    chunk = width // KVH
    feats = width // nd
    half = nz // 2
    stages = nz.bit_length() - 1
    vmem = pl.BlockSpec(memory_space=pltpu.VMEM)
    anywhere = pl.BlockSpec(memory_space=pl.ANY)
    dma = pltpu.SemaphoreType.DMA
    segments = jnp.tile(segment_ids[0], (1, per_group))
    gout, dk, dv, gg = pl.pallas_call(
        functools.partial(kernel, ns, nz),
        out_shape=(
            jax.ShapeDtypeStruct((micros, n_rows, width), bf16),
            jax.ShapeDtypeStruct((feats, kv_cols), f32),
            jax.ShapeDtypeStruct((feats, kv_cols), f32),
            jax.ShapeDtypeStruct((1, width), f32),
        ),
        in_specs=[vmem, vmem, vmem, vmem, vmem, anywhere, vmem, pl.BlockSpec(memory_space=pltpu.SMEM)],
        out_specs=(anywhere, vmem, vmem, vmem),
        scratch_shapes=[
            pltpu.VMEM((total, 128), f32),
            pltpu.VMEM((total, width), bf16),
            pltpu.VMEM((NY, nz * feats, total), bf16),
            pltpu.VMEM((nz * feats, NY * total), bf16),
            pltpu.VMEM((total, 2 * kv_cols), f32),
            pltpu.VMEM((total, 2 * kv_cols), bf16),
            pltpu.VMEM((micros, KVH, n_rows, n_rows * per_group), f32),
            pltpu.VMEM((kv_cols, width), bf16),
            pltpu.VMEM((kv_cols, width), bf16),
            pltpu.VMEM((micros, KVH, n_rows, chunk), bf16),
            pltpu.VMEM((micros, KVH, n_rows, chunk), bf16),
            pltpu.VMEM((NY * total, 2 * kv_cols), bf16),
            pltpu.VMEM((8, width), f32),
            pltpu.VMEM((NY, 8, width // 8), f32),
            pltpu.VMEM((stages, 8, width // 8), f32),
            pltpu.VMEM((stages, 8, width // 8), f32),
            pltpu.VMEM((2, half, 2, feats, kv_cols), bf16),
            pltpu.VMEM((2, half, 2, feats, kv_cols), bf16),
            dma((micros, KVH)),
            dma((micros, KVH)),
            dma((micros, KVH)),
            dma((micros, KVH)),
            dma((NY,)),
            dma((NY,)),
            dma,
            dma((NY, micros)),
            dma((NY, micros)),
            dma((NY,)),
            dma((NY,)),
            dma((stages,)),
            dma((stages,)),
            dma((2, half, 2)),
            dma((2, half, 2)),
        ],
        compiler_params=pltpu.CompilerParams(
            collective_id=0, has_side_effects=True, vmem_limit_bytes=48 * 2**20
        ),
        name="layers_backward",
    )(
        saved_inputs[0, 0].reshape(total, width),
        saved_queries[0, 0],
        norm_gain,
        key_weight[0],
        value_weight[0],
        out_cotangent[0],
        segments,
        token_counts[0],
    )
    return gout[None, None], dk[None], dv[None], gg


def solution(mesh):
    placed = (
        P("section", "dp", None, None, None),
        P("section", "dp", None, None, None),
        P("section", None),
        P("section", None, None),
        P("section", None, None),
        P("dp", None, None, None),
        P("dp", None),
        P("dp", None, None),
    )
    return jax.shard_map(
        functools.partial(shards, mesh.shape["section"], mesh.shape["dp"]),
        mesh=mesh,
        in_specs=placed,
        out_specs=(
            P("section", "dp", None, None, None),
            P("section", "dp", None),
            P("section", "dp", None),
            P("section", None),
        ),
        check_vma=False,
    )
```

```python
import functools

import jax
import jax.numpy as jnp
from jax import lax
from jax.experimental import pallas as pl
from jax.experimental.pallas import tpu as pltpu
from jax.sharding import PartitionSpec as P

HD = 128
KVH = 4
EPS = 1e-05
NY = 4
PARTS = 4

f32 = jnp.float32
bf16 = jnp.bfloat16
MESH = pl.DeviceIdType.MESH


def dot(a, b):
    return jnp.dot(a, b, preferred_element_type=f32)


def dot_t(a, b):
    return lax.dot_general(a, b, (((1,), (1,)), ((), ())), preferred_element_type=f32)


def aligned(index, size):
    return pl.ds(pl.multiple_of(index * size, size), size)


def heads(rows, count):
    return jnp.concatenate([rows[:, a * HD : (a + 1) * HD] for a in range(count)], axis=0)


def normalise(x, gain, inv, normed):
    width = x.shape[1]

    def step(r, _):
        rows = aligned(r, 16)
        xb = x[rows, :].astype(f32)
        scale = lax.rsqrt(jnp.sum(xb * xb, axis=1, keepdims=True) * (1.0 / width) + EPS)
        inv[rows, :] = jnp.broadcast_to(scale, (16, 128))
        normed[rows, :] = (xb * scale * gain[...]).astype(bf16)
        return _

    lax.fori_loop(0, x.shape[0] // 16, step, 0)


def project(c, parts, normed, weights, turned, kv32):
    depth = normed.shape[1] // parts
    rows = aligned(c, depth)
    features = normed[:, rows]
    for p, (w, wt) in enumerate(zip(weights, turned)):
        cols = slice(p * w.shape[1], (p + 1) * w.shape[1])
        block = w[rows, :]
        kv32[:, cols] += dot(features, block)
        wt[:, rows] = block.T


def probabilities(m, q, kvb, seg, counts, probs):
    n_rows, width = q.shape[1], q.shape[2]
    per_group = width // HD // KVH
    n = n_rows * per_group
    rows = aligned(m, n_rows)
    seg_row = seg[pl.ds(m, 1), :]
    seg_i = jnp.broadcast_to(jnp.concatenate([seg_row] * per_group, axis=1), (n_rows, n))
    micro = lax.broadcasted_iota(jnp.int32, counts.shape, 1)
    count = jnp.sum(jnp.where(micro == m, counts[...], 0), axis=1, keepdims=True)
    j = lax.broadcasted_iota(jnp.int32, (n_rows, n), 0)
    i = lax.rem(lax.broadcasted_iota(jnp.int32, (n_rows, n), 1), n_rows)
    seg_j = jnp.sum(jnp.where(i == j, seg_i, 0), axis=1, keepdims=True)
    allowed = ((j <= i) & (seg_i * per_group == seg_j) & (j < count)) | (i == j)
    for g in range(KVH):
        keys = kvb[rows, g * HD : (g + 1) * HD]
        queries = heads(q[m, :, g * per_group * HD : (g + 1) * per_group * HD], per_group)
        scores = dot_t(keys, queries) * (HD**-0.5)
        weights = jnp.where(allowed, jnp.exp(scores), 0.0)
        full = weights / jnp.sum(weights, axis=0, keepdims=True)
        probs[m, g] = jnp.where(i < count, full, 0.0)


def attend(m, g, incoming, q, kvb, probs, both):
    n_rows, width = q.shape[1], q.shape[2]
    per_group = width // HD // KVH
    kv_cols = KVH * HD
    rows = aligned(m, n_rows)
    values = kvb[rows, kv_cols + g * HD : kv_cols + (g + 1) * HD]
    head_grad = heads(incoming, per_group)
    queries = heads(q[m, :, g * per_group * HD : (g + 1) * per_group * HD], per_group)
    p = probs[m, g]
    prob_grad = dot_t(values, head_grad)
    score_grad = p * (prob_grad - jnp.sum(p * prob_grad, axis=0, keepdims=True)) * (HD**-0.5)
    both[rows, kv_cols + g * HD : kv_cols + (g + 1) * HD] = dot(p.astype(bf16), head_grad).astype(bf16)
    both[rows, g * HD : (g + 1) * HD] = dot(score_grad.astype(bf16), queries).astype(bf16)


def kernel(
    ns, nz, x_in, q_in, gain_in, kw_in, vw_in, cot, seg_in, counts_in,
    gout, dk, dv, gg,
    x, q, gain, kw, vw, seg, counts, inv, normed, normed_t, normed_all, kv32, kvb, probs, kwt, vwt,
    gin, gnext, grads, gacc, gain_y, gain_zs, gain_zr, ring_s, ring_r,
    x_sem, q_sem, gain_sem, seg_sem, counts_sem, w_sem, cot_sem, next_s, next_r, out_sem, nt_s, nt_r, nt_l, kv_s, kv_r, gy_s, gy_r, gz_s, gz_r, ring_ss, ring_rs,
):
    micros, n_rows, width = q.shape
    parts = w_sem.shape[1]
    total = micros * n_rows
    kv_cols = kw.shape[1]
    chunk = width // KVH
    feats = width // (nz * NY)
    sec = lax.axis_index("section")
    dp = lax.axis_index("dp")
    z, y = lax.div(dp, NY), lax.rem(dp, NY)
    is_last = sec == ns - 1
    stages = nz.bit_length() - 1
    half = nz // 2

    def along_z(k):
        return lax.rem(z + k + nz, nz)

    def along_y(k):
        return lax.rem(y + k, NY)

    def flipped(b):
        return z + b - 2 * b * lax.rem(lax.div(z, b), 2)

    def device(zz, yy):
        return (sec, zz * NY + yy)

    y_peers = [device(z, along_y(k)) for k in range(1, NY)]
    up, down = device(along_z(1), y), device(along_z(-1), y)
    flips = [device(flipped(1 << i), y) for i in range(stages)]

    def remote(src, dst, ssem, rsem, dev):
        return pltpu.make_async_remote_copy(
            src_ref=src, dst_ref=dst, send_sem=ssem, recv_sem=rsem, device_id=dev, device_id_type=MESH
        )

    def w_copy(p, c):
        rows = aligned(c, width // parts)
        return pltpu.make_async_copy((kw_in, vw_in)[p].at[rows, :], (kw, vw)[p].at[rows, :], w_sem.at[p, c])

    x_copy = pltpu.make_async_copy(x_in, x, x_sem)
    q_copy = pltpu.make_async_copy(q_in, q, q_sem)
    gain_copy = pltpu.make_async_copy(gain_in, gain, gain_sem)
    seg_copy = pltpu.make_async_copy(seg_in, seg, seg_sem)
    counts_copy = pltpu.make_async_copy(counts_in, counts, counts_sem)
    x_copy.start()
    gain_copy.start()
    for c in range(parts):
        for p in range(2):
            w_copy(p, c).start()
        if c == 0:
            q_copy.start()
            seg_copy.start()
            counts_copy.start()

    barrier = pltpu.get_barrier_semaphore()
    above, below = (lax.rem(sec + 1, ns), dp), (lax.rem(sec + ns - 1, ns), dp)
    greeted = y_peers + [up, down] + flips[1:] + [above, below]
    for peer in greeted:
        pl.semaphore_signal(barrier, inc=1, device_id=peer, device_id_type=MESH)

    def cot_copy(m, g):
        return pltpu.make_async_copy(
            cot.at[m, :, pl.ds(g * chunk, chunk)], gin.at[1, m, g], cot_sem.at[m, g]
        )

    @pl.when(is_last)
    def _():
        for m in range(micros):
            for g in range(KVH):
                cot_copy(m, g).start()

    kv32[...] = jnp.zeros_like(kv32)
    gacc[...] = jnp.zeros_like(gacc)
    x_copy.wait()
    gain_copy.wait()
    normalise(x, gain, inv, normed)

    def each_part(c, carry):
        for p in range(2):
            w_copy(p, c).wait()
        project(c, parts, normed, (kw, vw), (kwt, vwt), kv32)
        return carry

    lax.fori_loop(0, parts, each_part, 0)
    kvb[...] = kv32[...].astype(bf16)
    q_copy.wait()
    seg_copy.wait()
    counts_copy.wait()

    def each_probs(m, carry):
        probabilities(m, q, kvb, seg, counts, probs)
        return carry

    def turn(b, carry):
        first = b * 128
        owner = lax.div(first, feats)
        at = lax.div(owner, NY) * feats + lax.rem(first, feats)
        normed_t[lax.rem(owner, NY), pl.ds(pl.multiple_of(at, 128), 128), :] = normed[:, aligned(b, 128)].T
        return carry

    pl.semaphore_wait(barrier, len(greeted))

    def nt_copy(k):
        return remote(
            normed_t.at[along_y(k)], normed_all.at[:, pl.ds(k * total, total)], nt_s.at[k], nt_r.at[k], y_peers[k - 1]
        )

    own_nt = pltpu.make_async_copy(normed_t.at[y], normed_all.at[:, pl.ds(0, total)], nt_l)

    def exchange_normed():
        lax.fori_loop(0, width // 128, turn, 0)
        for k in range(1, NY):
            nt_copy(k).start()
        own_nt.start()

    def next_copy(m, g):
        return remote(gnext.at[m, g], gin.at[0, m, g], next_s.at[m, g], next_r.at[m, g], below)

    def out_copy(m, g):
        return pltpu.make_async_copy(
            gnext.at[m, g], gout.at[m, :, pl.ds(g * chunk, chunk)], out_sem.at[m, g]
        )

    def kv_copy(m, k):
        rows = aligned(m, n_rows)
        to = pl.ds(pl.multiple_of(k * total + m * n_rows, n_rows), n_rows)
        return remote(grads.at[rows, :], grads.at[to, :], kv_s.at[k, m], kv_r.at[k, m], y_peers[k - 1])

    def layer(last, m, carry):
        incoming = gin.at[int(last)]
        if last:
            probabilities(m, q, kvb, seg, counts, probs)
        for g in range(KVH):
            if last:
                cot_copy(m, g).wait()
            else:
                next_copy(m, g).wait_recv()
            attend(m, g, incoming[m, g], q, kvb, probs, grads)
        for k in range(1, NY):
            kv_copy(m, k).start()
        rows = aligned(m, n_rows)
        both = grads[rows, :]
        scale = inv[rows, 0:1]
        pulled = jnp.sum(both.astype(f32) * kv32[rows, :], axis=1, keepdims=True) * (
            scale * scale * (1.0 / width)
        )
        for g in range(KVH):
            cols = slice(g * chunk, (g + 1) * chunk)
            grad = (dot(both[:, :kv_cols], kwt[:, cols]) + dot(both[:, kv_cols:], vwt[:, cols])) * scale
            xb = x[rows, cols].astype(f32)
            gnext[m, g] = (incoming[m, g].astype(f32) + grad * gain[:, cols] - xb * pulled).astype(bf16)
            next_copy(m, g).start()
            term = grad * xb
            gacc[:, cols] += term[0:8] + term[8:16] + term[16:24] + term[24:32]
        for g in range(KVH):
            out_copy(m, g).start()
        return carry

    @pl.when(is_last)
    def _():
        lax.fori_loop(0, micros, functools.partial(layer, True), 0)
        exchange_normed()

    @pl.when(jnp.logical_not(is_last))
    def _():
        lax.fori_loop(0, micros, each_probs, 0)
        exchange_normed()
        lax.fori_loop(0, micros, functools.partial(layer, False), 0)

    part = width // 8
    gsum = jnp.sum(gacc[...], axis=0, keepdims=True)
    for r in range(8):
        gain_y[0, r : r + 1, :] = gsum[:, r * part : (r + 1) * part]

    def gy_copy(k):
        return remote(gain_y.at[0], gain_y.at[k], gy_s.at[k], gy_r.at[k], y_peers[k - 1])

    def gz_copy(i):
        return remote(gain_zs.at[i], gain_zr.at[i], gz_s.at[i], gz_r.at[i], flips[i])

    for k in range(1, NY):
        gy_copy(k).start()

    def gain_stage(i):
        if i == 0:
            for k in range(1, NY):
                gy_copy(k).wait_recv()
            summed = gain_y[0]
            for k in range(1, NY):
                summed = summed + gain_y[k]
        else:
            gz_copy(i - 1).wait_recv()
            summed = gain_zs[i - 1] + gain_zr[i - 1]
        if i < stages:
            gain_zs[i] = summed
            gz_copy(i).start()
        else:
            for r in range(8):
                gg[:, r * part : (r + 1) * part] = summed[r : r + 1, :]

    own_nt.wait()
    for k in range(1, NY):
        nt_copy(k).wait_recv()

    def kv_waits(m, _):
        for k in range(1, NY):
            kv_copy(m, k).wait_recv()
        return _

    lax.fori_loop(0, micros, kv_waits, 0)

    def piece(zz, h):
        return dot(normed_all[aligned(zz, feats), :], grads[:, h * kv_cols : (h + 1) * kv_cols])

    def ring_copy(way, t, h):
        return remote(
            ring_s.at[way, t, h], ring_r.at[way, t, h], ring_ss.at[way, t, h], ring_rs.at[way, t, h],
            (down, up)[way],
        )

    for t in range(half):
        sums = {}
        for way in range(2):
            target = along_z((t - half) if way == 0 else (half - t))
            for h in range(2):
                if t > 0 or h == way:
                    sums[way, h] = piece(target, h)
        for h in range(2):
            for way in range(2):
                if (way, h) in sums:
                    value = sums[way, h]
                    if t > 1 or (t == 1 and h == way):
                        ring_copy(way, t - 1, h).wait_recv()
                        value = value + ring_r[way, t - 1, h].astype(f32)
                    ring_s[way, t, h] = value.astype(bf16)
                    ring_copy(way, t, h).start()
        if t <= stages:
            gain_stage(t)
    for t in range(half, stages + 1):
        gain_stage(t)
    own = [piece(z, h) for h in range(2)]
    for h, out in enumerate((dk, dv)):
        value = own[h]
        for way in range(2):
            ring_copy(way, half - 1, h).wait_recv()
            value = value + ring_r[way, half - 1, h].astype(f32)
        out[...] = value

    def sent(m, carry):
        for g in range(KVH):
            next_copy(m, g).wait_send()
            out_copy(m, g).wait()
        for k in range(1, NY):
            kv_copy(m, k).wait_send()
        return carry

    lax.fori_loop(0, micros, sent, 0)
    for k in range(1, NY):
        nt_copy(k).wait_send()
        gy_copy(k).wait_send()

    @pl.when(is_last)
    def _():
        for m in range(micros):
            for g in range(KVH):
                next_copy(m, g).wait_recv()

    for i in range(stages):
        gz_copy(i).wait_send()
    for t in range(half):
        for way in range(2):
            for h in range(2):
                if t > 0 or h == way:
                    ring_copy(way, t, h).wait_send()


def store(*refs):
    count = len(refs) // 2
    copies = [pltpu.make_async_copy(refs[r], refs[count + r], refs[-1].at[r]) for r in range(count)]
    for copy in copies:
        copy.start()
    for copy in copies:
        copy.wait()


def shards(ns, nd, saved_inputs, saved_queries, norm_gain, key_weight, value_weight, out_cotangent, token_counts, segment_ids):
    micros, n_rows, width = saved_inputs.shape[2:]
    kv_cols = key_weight.shape[2]
    total = micros * n_rows
    nz = nd // NY
    per_group = width // HD // KVH
    chunk = width // KVH
    feats = width // nd
    half = nz // 2
    stages = nz.bit_length() - 1
    vmem = pl.BlockSpec(memory_space=pltpu.VMEM)
    hbm = pl.BlockSpec(memory_space=pltpu.HBM)
    dma = pltpu.SemaphoreType.DMA
    gout, dk, dv, gg = pl.pallas_call(
        functools.partial(kernel, ns, nz),
        out_shape=(
            jax.ShapeDtypeStruct((micros, n_rows, width), bf16),
            jax.ShapeDtypeStruct((feats, kv_cols), f32),
            jax.ShapeDtypeStruct((feats, kv_cols), f32),
            jax.ShapeDtypeStruct((1, width), f32),
        ),
        in_specs=[hbm] * 8,
        out_specs=(hbm, vmem, vmem, vmem),
        scratch_shapes=[
            pltpu.VMEM((total, width), bf16),
            pltpu.VMEM((micros, n_rows, width), bf16),
            pltpu.VMEM((1, width), f32),
            pltpu.VMEM((width, kv_cols), bf16),
            pltpu.VMEM((width, kv_cols), bf16),
            pltpu.VMEM((micros, n_rows), jnp.int32),
            pltpu.VMEM((1, micros), jnp.int32),
            pltpu.VMEM((total, 128), f32),
            pltpu.VMEM((total, width), bf16),
            pltpu.VMEM((NY, nz * feats, total), bf16),
            pltpu.VMEM((nz * feats, NY * total), bf16),
            pltpu.VMEM((total, 2 * kv_cols), f32),
            pltpu.VMEM((total, 2 * kv_cols), bf16),
            pltpu.VMEM((micros, KVH, n_rows, n_rows * per_group), f32),
            pltpu.VMEM((kv_cols, width), bf16),
            pltpu.VMEM((kv_cols, width), bf16),
            pltpu.VMEM((2, micros, KVH, n_rows, chunk), bf16),
            pltpu.VMEM((micros, KVH, n_rows, chunk), bf16),
            pltpu.VMEM((NY * total, 2 * kv_cols), bf16),
            pltpu.VMEM((8, width), f32),
            pltpu.VMEM((NY, 8, width // 8), f32),
            pltpu.VMEM((stages, 8, width // 8), f32),
            pltpu.VMEM((stages, 8, width // 8), f32),
            pltpu.VMEM((2, half, 2, feats, kv_cols), bf16),
            pltpu.VMEM((2, half, 2, feats, kv_cols), bf16),
            dma,
            dma,
            dma,
            dma,
            dma,
            dma((2, PARTS)),
            dma((micros, KVH)),
            dma((micros, KVH)),
            dma((micros, KVH)),
            dma((micros, KVH)),
            dma((NY,)),
            dma((NY,)),
            dma,
            dma((NY, micros)),
            dma((NY, micros)),
            dma((NY,)),
            dma((NY,)),
            dma((stages,)),
            dma((stages,)),
            dma((2, half, 2)),
            dma((2, half, 2)),
        ],
        compiler_params=pltpu.CompilerParams(
            collective_id=0, has_side_effects=True, vmem_limit_bytes=60 * 2**20
        ),
        name="layers_backward",
    )(
        saved_inputs[0, 0].reshape(total, width),
        saved_queries[0, 0],
        norm_gain,
        key_weight[0],
        value_weight[0],
        out_cotangent[0],
        segment_ids[0],
        token_counts,
    )
    results = (gout, dk, dv, gg)
    gout, dk, dv, gg = pl.pallas_call(
        store,
        out_shape=tuple(jax.ShapeDtypeStruct(r.shape, r.dtype) for r in results),
        in_specs=[vmem] * len(results),
        out_specs=(hbm,) * len(results),
        scratch_shapes=[dma((len(results),))],
        compiler_params=pltpu.CompilerParams(vmem_limit_bytes=60 * 2**20),
        name="store_results",
    )(*results)
    return gout[None, None], dk[None], dv[None], gg


def solution(mesh):
    placed = (
        P("section", "dp", None, None, None),
        P("section", "dp", None, None, None),
        P("section", None),
        P("section", None, None),
        P("section", None, None),
        P("dp", None, None, None),
        P("dp", None),
        P("dp", None, None),
    )
    return jax.shard_map(
        functools.partial(shards, mesh.shape["section"], mesh.shape["dp"]),
        mesh=mesh,
        in_specs=placed,
        out_specs=(
            P("section", "dp", None, None, None),
            P("section", "dp", None),
            P("section", "dp", None),
            P("section", None),
        ),
        check_vma=False,
    )
```

```python
import functools

import jax
import jax.numpy as jnp
from jax import lax
from jax.experimental import pallas as pl
from jax.experimental.pallas import tpu as pltpu
from jax.sharding import PartitionSpec as P

HD = 128
KVH = 4
EPS = 1e-05
NY = 4
PARTS = 4
SLICES = 6
Z_GROUPS = 2

f32 = jnp.float32
bf16 = jnp.bfloat16
MESH = pl.DeviceIdType.MESH


def dot(a, b):
    return jnp.dot(a, b, preferred_element_type=f32)


def dot_t(a, b):
    return lax.dot_general(a, b, (((1,), (1,)), ((), ())), preferred_element_type=f32)


def aligned(index, size):
    return pl.ds(pl.multiple_of(index * size, size), size)


def heads(rows, count):
    return jnp.concatenate([rows[:, a * HD : (a + 1) * HD] for a in range(count)], axis=0)


def normalise(x, gain, inv, normed):
    width = x.shape[1]

    def step(r, _):
        rows = aligned(r, 16)
        xb = x[rows, :].astype(f32)
        scale = lax.rsqrt(jnp.sum(xb * xb, axis=1, keepdims=True) * (1.0 / width) + EPS)
        inv[rows, :] = jnp.broadcast_to(scale, (16, 128))
        normed[rows, :] = (xb * scale * gain[...]).astype(bf16)
        return _

    lax.fori_loop(0, x.shape[0] // 16, step, 0)


def project(c, parts, normed, weights, turned, kv32):
    depth = normed.shape[1] // parts
    rows = aligned(c, depth)
    features = normed[:, rows]
    for p, (w, wt) in enumerate(zip(weights, turned)):
        cols = slice(p * w.shape[1], (p + 1) * w.shape[1])
        block = w[rows, :]
        kv32[:, cols] += dot(features, block)
        wt[:, rows] = block.T


def probabilities(m, q, kvb, seg, counts, probs):
    n_rows, width = q.shape[1], q.shape[2]
    per_group = width // HD // KVH
    n = n_rows * per_group
    rows = aligned(m, n_rows)
    seg_row = seg[pl.ds(m, 1), :]
    seg_i = jnp.broadcast_to(jnp.concatenate([seg_row] * per_group, axis=1), (n_rows, n))
    micro = lax.broadcasted_iota(jnp.int32, counts.shape, 1)
    count = jnp.sum(jnp.where(micro == m, counts[...], 0), axis=1, keepdims=True)
    j = lax.broadcasted_iota(jnp.int32, (n_rows, n), 0)
    i = lax.rem(lax.broadcasted_iota(jnp.int32, (n_rows, n), 1), n_rows)
    seg_j = jnp.sum(jnp.where(i == j, seg_i, 0), axis=1, keepdims=True)
    allowed = ((j <= i) & (seg_i * per_group == seg_j) & (j < count)) | (i == j)
    for g in range(KVH):
        keys = kvb[rows, g * HD : (g + 1) * HD]
        queries = heads(q[m, :, g * per_group * HD : (g + 1) * per_group * HD], per_group)
        scores = dot_t(keys, queries) * (HD**-0.5)
        weights = jnp.where(allowed, jnp.exp(scores), 0.0)
        full = weights / jnp.sum(weights, axis=0, keepdims=True)
        probs[m, g] = jnp.where(i < count, full, 0.0)


def attend(m, g, incoming, q, kvb, probs, zgrads, ygrads):
    n_rows, width = q.shape[1], q.shape[2]
    per_group = width // HD // KVH
    kv_cols = KVH * HD
    rows = aligned(m, n_rows)
    values = kvb[rows, kv_cols + g * HD : kv_cols + (g + 1) * HD]
    head_grad = heads(incoming, per_group)
    queries = heads(q[m, :, g * per_group * HD : (g + 1) * per_group * HD], per_group)
    p = probs[m, g]
    prob_grad = dot_t(values, head_grad)
    score_grad = p * (prob_grad - jnp.sum(p * prob_grad, axis=0, keepdims=True)) * (HD**-0.5)
    key_grad = dot(score_grad.astype(bf16), queries).astype(bf16)
    first = (KVH - Z_GROUPS + g) * HD
    ygrads[rows, first : first + HD] = dot(p.astype(bf16), head_grad).astype(bf16)
    if g < Z_GROUPS:
        zgrads[rows, g * HD : (g + 1) * HD] = key_grad
    else:
        ygrads[rows, (g - Z_GROUPS) * HD : (g - Z_GROUPS + 1) * HD] = key_grad


def kernel(
    ns, nz, x_in, q_in, gain_in, kw_in, vw_in, cot, seg_in, counts_in,
    gout, dk, dv, gg,
    x, q, gain, kw, vw, seg, counts, inv, normed, normed_y, all_y, normed_z, all_z, kv32, kvb, probs, kwt, vwt,
    gin, gnext, zgrads, ygrads, gacc, gain_y, gain_zs, gain_zr, pieces, ring_s, ring_r, key_s, key_r,
    x_sem, q_sem, gain_sem, seg_sem, counts_sem, w_sem, cot_sem, next_s, next_r, out_sem, ny_s, ny_r, ny_l, nz_s, nz_r, nz_l, gy2_s, gy2_r, gz2_s, gz2_r, ks_s, ks_r, gy_s, gy_r, gz_s, gz_r, ring_ss, ring_rs,
):
    micros, n_rows, width = q.shape
    parts = w_sem.shape[1]
    total = micros * n_rows
    kv_cols = kw.shape[1]
    chunk = width // KVH
    feats = width // (nz * NY)
    sec = lax.axis_index("section")
    dp = lax.axis_index("dp")
    z, y = lax.div(dp, NY), lax.rem(dp, NY)
    is_last = sec == ns - 1
    stages = nz.bit_length() - 1
    half = nz // 2

    def along_z(k):
        return lax.rem(z + k + nz, nz)

    def along_y(k):
        return lax.rem(y + k, NY)

    def flipped(b):
        return z + b - 2 * b * lax.rem(lax.div(z, b), 2)

    def device(zz, yy):
        return (sec, zz * NY + yy)

    y_peers = [device(z, along_y(k)) for k in range(1, NY)]
    up, down = device(along_z(1), y), device(along_z(-1), y)
    z_peers = [device(along_z(k), y) for k in range(1, nz)]
    flips = [device(flipped(1 << i), y) for i in range(stages)]

    def remote(src, dst, ssem, rsem, dev):
        return pltpu.make_async_remote_copy(
            src_ref=src, dst_ref=dst, send_sem=ssem, recv_sem=rsem, device_id=dev, device_id_type=MESH
        )

    def w_copy(p, c):
        rows = aligned(c, width // parts)
        return pltpu.make_async_copy((kw_in, vw_in)[p].at[rows, :], (kw, vw)[p].at[rows, :], w_sem.at[p, c])

    x_copy = pltpu.make_async_copy(x_in, x, x_sem)
    q_copy = pltpu.make_async_copy(q_in, q, q_sem)
    gain_copy = pltpu.make_async_copy(gain_in, gain, gain_sem)
    seg_copy = pltpu.make_async_copy(seg_in, seg, seg_sem)
    counts_copy = pltpu.make_async_copy(counts_in, counts, counts_sem)
    x_copy.start()
    gain_copy.start()
    for c in range(parts):
        for p in range(2):
            w_copy(p, c).start()
        if c == 0:
            q_copy.start()
            seg_copy.start()
            counts_copy.start()

    barrier = pltpu.get_barrier_semaphore()
    above, below = (lax.rem(sec + 1, ns), dp), (lax.rem(sec + ns - 1, ns), dp)
    greeted = y_peers + z_peers + [above, below]
    for peer in greeted:
        pl.semaphore_signal(barrier, inc=1, device_id=peer, device_id_type=MESH)

    def cot_copy(g):
        return pltpu.make_async_copy(cot.at[:, :, pl.ds(g * chunk, chunk)], gin.at[1, :, g], cot_sem.at[g])

    @pl.when(is_last)
    def _():
        for g in range(KVH):
            cot_copy(g).start()

    kv32[...] = jnp.zeros_like(kv32)
    gacc[...] = jnp.zeros_like(gacc)
    x_copy.wait()
    gain_copy.wait()
    normalise(x, gain, inv, normed)

    def each_part(c, carry):
        for p in range(2):
            w_copy(p, c).wait()
        project(c, parts, normed, (kw, vw), (kwt, vwt), kv32)
        return carry

    lax.fori_loop(0, parts, each_part, 0)
    kvb[...] = kv32[...].astype(bf16)
    q_copy.wait()
    seg_copy.wait()
    counts_copy.wait()

    def each_probs(m, carry):
        probabilities(m, q, kvb, seg, counts, probs)
        return carry

    def turn(b, carry):
        first = b * 128
        owner = lax.div(first, feats)
        oz, oy, offset = lax.div(owner, NY), lax.rem(owner, NY), lax.rem(first, feats)
        block = normed[:, aligned(b, 128)].T
        normed_y[oy, pl.ds(pl.multiple_of(oz * feats + offset, 128), 128), :] = block
        normed_z[oz, pl.ds(pl.multiple_of(oy * feats + offset, 128), 128), :] = block
        return carry

    pl.semaphore_wait(barrier, len(greeted))

    def ny_copy(k):
        return remote(normed_y.at[along_y(k)], all_y.at[:, pl.ds(k * total, total)], ny_s.at[k], ny_r.at[k], y_peers[k - 1])

    def nz_copy(k):
        return remote(normed_z.at[along_z(k)], all_z.at[:, pl.ds(k * total, total)], nz_s.at[k], nz_r.at[k], z_peers[k - 1])

    own_ny = pltpu.make_async_copy(normed_y.at[y], all_y.at[:, pl.ds(0, total)], ny_l)
    own_nz = pltpu.make_async_copy(normed_z.at[z], all_z.at[:, pl.ds(0, total)], nz_l)

    def exchange_normed():
        lax.fori_loop(0, width // 128, turn, 0)
        for k in range(1, NY):
            ny_copy(k).start()
        for k in range(1, nz):
            nz_copy(k).start()
        own_ny.start()
        own_nz.start()

    def next_copy(m, g):
        return remote(gnext.at[m, g], gin.at[0, m, g], next_s.at[m, g], next_r.at[m, g], below)

    def out_copy(g):
        return pltpu.make_async_copy(gnext.at[:, g], gout.at[:, :, pl.ds(g * chunk, chunk)], out_sem.at[g])

    def rows_of(m, k):
        return pl.ds(pl.multiple_of(k * total + m * n_rows, n_rows), n_rows)

    def yg_copy(m, k):
        return remote(ygrads.at[rows_of(m, 0), :], ygrads.at[rows_of(m, k), :], gy2_s.at[k, m], gy2_r.at[k, m], y_peers[k - 1])

    def zg_copy(m, k):
        return remote(zgrads.at[rows_of(m, 0), :], zgrads.at[rows_of(m, k), :], gz2_s.at[k, m], gz2_r.at[k, m], z_peers[k - 1])

    def layer(last, m, carry):
        incoming = gin.at[int(last)]
        if last:
            probabilities(m, q, kvb, seg, counts, probs)
        for g in range(KVH):
            if not last:
                next_copy(m, g).wait_recv()
            attend(m, g, incoming[m, g], q, kvb, probs, zgrads, ygrads)
        rows = aligned(m, n_rows)
        split = kv_cols - Z_GROUPS * HD
        kg = jnp.concatenate([zgrads[rows, :], ygrads[rows, :split]], axis=1)
        vg = ygrads[rows, split:]
        scale = inv[rows, 0:1]
        along = kg.astype(f32) * kv32[rows, :kv_cols] + vg.astype(f32) * kv32[rows, kv_cols:]
        pulled = jnp.sum(along, axis=1, keepdims=True) * (scale * scale * (1.0 / width))
        for g in range(KVH):
            cols = slice(g * chunk, (g + 1) * chunk)
            grad = (dot(kg, kwt[:, cols]) + dot(vg, vwt[:, cols])) * scale
            xb = x[rows, cols].astype(f32)
            gnext[m, g] = (incoming[m, g].astype(f32) + grad * gain[:, cols] - xb * pulled).astype(bf16)
            next_copy(m, g).start()
            if g == 0:
                for k in range(1, NY):
                    yg_copy(m, k).start()
                for k in range(1, nz):
                    zg_copy(m, k).start()
            term = grad * xb
            gacc[:, cols] += term[0:8] + term[8:16] + term[16:24] + term[24:32]
        return carry

    @pl.when(is_last)
    def _():
        for g in range(KVH):
            cot_copy(g).wait()
        lax.fori_loop(0, micros, functools.partial(layer, True), 0)
        exchange_normed()

    @pl.when(jnp.logical_not(is_last))
    def _():
        lax.fori_loop(0, micros, each_probs, 0)
        exchange_normed()
        lax.fori_loop(0, micros, functools.partial(layer, False), 0)

    for g in range(KVH):
        out_copy(g).start()

    part = width // 8
    gsum = jnp.sum(gacc[...], axis=0, keepdims=True)
    for r in range(8):
        gain_y[0, r : r + 1, :] = gsum[:, r * part : (r + 1) * part]

    def gy_copy(k):
        return remote(gain_y.at[0], gain_y.at[k], gy_s.at[k], gy_r.at[k], y_peers[k - 1])

    def gz_copy(i):
        return remote(gain_zs.at[i], gain_zr.at[i], gz_s.at[i], gz_r.at[i], flips[i])

    for k in range(1, NY):
        gy_copy(k).start()

    def gain_stage(i):
        if i == 0:
            for k in range(1, NY):
                gy_copy(k).wait_recv()
            summed = gain_y[0]
            for k in range(1, NY):
                summed = summed + gain_y[k]
        else:
            gz_copy(i - 1).wait_recv()
            summed = gain_zs[i - 1] + gain_zr[i - 1]
        if i < stages:
            gain_zs[i] = summed
            gz_copy(i).start()
        else:
            for r in range(8):
                gg[:, r * part : (r + 1) * part] = summed[r : r + 1, :]

    own_ny.wait()
    for k in range(1, NY):
        ny_copy(k).wait_recv()

    def yg_waits(m, carry):
        for k in range(1, NY):
            yg_copy(m, k).wait_recv()
        return carry

    lax.fori_loop(0, micros, yg_waits, 0)
    slice_cols = ygrads.shape[1] // SLICES

    def each_piece(k, carry):
        pieces[k] = dot(all_y[aligned(along_z(k), feats), :], ygrads[...])
        return carry

    def piece(k, h):
        return pieces[k % nz, :, h * slice_cols : (h + 1) * slice_cols]

    def key_piece(yy):
        return dot(all_z[aligned(yy, feats), :], zgrads[...])

    def key_copy(k):
        return remote(key_s.at[k], key_r.at[k], ks_s.at[k], ks_r.at[k], y_peers[k - 1])

    def zg_waits(m, carry):
        for k in range(1, nz):
            zg_copy(m, k).wait_recv()
        return carry

    def key_send():
        own_nz.wait()
        for k in range(1, nz):
            nz_copy(k).wait_recv()
        lax.fori_loop(0, micros, zg_waits, 0)
        for k in range(1, NY):
            key_s[k] = key_piece(along_y(k)).astype(bf16)
            key_copy(k).start()
        dk[:, : Z_GROUPS * HD] = key_piece(y)

    def ring_copy(way, t, h):
        return remote(
            ring_s.at[way, t, h], ring_r.at[way, t, h], ring_ss.at[way, t, h], ring_rs.at[way, t, h],
            (down, up)[way],
        )

    def in_ring(way, t, h):
        return t > 0 or (t == 0 and h * 2 // SLICES == way)

    each_piece(half, 0)
    for t in range(half):
        for h in range(SLICES):
            for way in range(2):
                if in_ring(way, t, h):
                    value = piece((t - half) if way == 0 else (half - t), h)
                    if in_ring(way, t - 1, h):
                        ring_copy(way, t - 1, h).wait_recv()
                        value = value + ring_r[way, t - 1, h].astype(f32)
                    ring_s[way, t, h] = value.astype(bf16)
                    ring_copy(way, t, h).start()
        if t == 0:
            lax.fori_loop(1, half, each_piece, 0)
            lax.fori_loop(half + 1, nz, each_piece, 0)
            each_piece(0, 0)
            key_send()
        if t <= stages:
            gain_stage(t)
    for t in range(half, stages + 1):
        gain_stage(t)
    for h in range(SLICES):
        value = piece(0, h)
        for way in range(2):
            ring_copy(way, half - 1, h).wait_recv()
            value = value + ring_r[way, half - 1, h].astype(f32)
        first = Z_GROUPS * HD + h * slice_cols
        out = (dk, dv)[first // kv_cols]
        out[:, first % kv_cols : first % kv_cols + slice_cols] = value
    for k in range(1, NY):
        key_copy(k).wait_recv()
        dk[:, : Z_GROUPS * HD] += key_r[k].astype(f32)

    def sent(m, carry):
        for g in range(KVH):
            next_copy(m, g).wait_send()
        for k in range(1, NY):
            yg_copy(m, k).wait_send()
        for k in range(1, nz):
            zg_copy(m, k).wait_send()
        return carry

    for g in range(KVH):
        out_copy(g).wait()
    lax.fori_loop(0, micros, sent, 0)
    for k in range(1, NY):
        ny_copy(k).wait_send()
        gy_copy(k).wait_send()
        key_copy(k).wait_send()
    for k in range(1, nz):
        nz_copy(k).wait_send()

    @pl.when(is_last)
    def _():
        for m in range(micros):
            for g in range(KVH):
                next_copy(m, g).wait_recv()

    for i in range(stages):
        gz_copy(i).wait_send()
    for t in range(half):
        for way in range(2):
            for h in range(SLICES):
                if in_ring(way, t, h):
                    ring_copy(way, t, h).wait_send()


def store(*refs):
    count = len(refs) // 2
    copies = [pltpu.make_async_copy(refs[r], refs[count + r], refs[-1].at[r]) for r in range(count)]
    for copy in copies:
        copy.start()
    for copy in copies:
        copy.wait()


def shards(ns, nd, saved_inputs, saved_queries, norm_gain, key_weight, value_weight, out_cotangent, token_counts, segment_ids):
    micros, n_rows, width = saved_inputs.shape[2:]
    kv_cols = key_weight.shape[2]
    total = micros * n_rows
    nz = nd // NY
    per_group = width // HD // KVH
    chunk = width // KVH
    feats = width // nd
    half = nz // 2
    stages = nz.bit_length() - 1
    z_cols = Z_GROUPS * HD
    y_cols = 2 * kv_cols - z_cols
    vmem = pl.BlockSpec(memory_space=pltpu.VMEM)
    hbm = pl.BlockSpec(memory_space=pltpu.HBM)
    dma = pltpu.SemaphoreType.DMA
    gout, dk, dv, gg = pl.pallas_call(
        functools.partial(kernel, ns, nz),
        out_shape=(
            jax.ShapeDtypeStruct((micros, n_rows, width), bf16),
            jax.ShapeDtypeStruct((feats, kv_cols), f32),
            jax.ShapeDtypeStruct((feats, kv_cols), f32),
            jax.ShapeDtypeStruct((1, width), f32),
        ),
        in_specs=[hbm] * 8,
        out_specs=(hbm, vmem, vmem, vmem),
        scratch_shapes=[
            pltpu.VMEM((total, width), bf16),
            pltpu.VMEM((micros, n_rows, width), bf16),
            pltpu.VMEM((1, width), f32),
            pltpu.VMEM((width, kv_cols), bf16),
            pltpu.VMEM((width, kv_cols), bf16),
            pltpu.VMEM((micros, n_rows), jnp.int32),
            pltpu.VMEM((1, micros), jnp.int32),
            pltpu.VMEM((total, 128), f32),
            pltpu.VMEM((total, width), bf16),
            pltpu.VMEM((NY, nz * feats, total), bf16),
            pltpu.VMEM((nz * feats, NY * total), bf16),
            pltpu.VMEM((nz, NY * feats, total), bf16),
            pltpu.VMEM((NY * feats, nz * total), bf16),
            pltpu.VMEM((total, 2 * kv_cols), f32),
            pltpu.VMEM((total, 2 * kv_cols), bf16),
            pltpu.VMEM((micros, KVH, n_rows, n_rows * per_group), f32),
            pltpu.VMEM((kv_cols, width), bf16),
            pltpu.VMEM((kv_cols, width), bf16),
            pltpu.VMEM((2, micros, KVH, n_rows, chunk), bf16),
            pltpu.VMEM((micros, KVH, n_rows, chunk), bf16),
            pltpu.VMEM((nz * total, z_cols), bf16),
            pltpu.VMEM((NY * total, y_cols), bf16),
            pltpu.VMEM((8, width), f32),
            pltpu.VMEM((NY, 8, width // 8), f32),
            pltpu.VMEM((stages, 8, width // 8), f32),
            pltpu.VMEM((stages, 8, width // 8), f32),
            pltpu.VMEM((nz, feats, y_cols), f32),
            pltpu.VMEM((2, half, SLICES, feats, y_cols // SLICES), bf16),
            pltpu.VMEM((2, half, SLICES, feats, y_cols // SLICES), bf16),
            pltpu.VMEM((NY, feats, z_cols), bf16),
            pltpu.VMEM((NY, feats, z_cols), bf16),
            dma,
            dma,
            dma,
            dma,
            dma,
            dma((2, PARTS)),
            dma((KVH,)),
            dma((micros, KVH)),
            dma((micros, KVH)),
            dma((KVH,)),
            dma((NY,)),
            dma((NY,)),
            dma,
            dma((nz,)),
            dma((nz,)),
            dma,
            dma((NY, micros)),
            dma((NY, micros)),
            dma((nz, micros)),
            dma((nz, micros)),
            dma((NY,)),
            dma((NY,)),
            dma((NY,)),
            dma((NY,)),
            dma((stages,)),
            dma((stages,)),
            dma((2, half, SLICES)),
            dma((2, half, SLICES)),
        ],
        compiler_params=pltpu.CompilerParams(
            collective_id=0, has_side_effects=True, vmem_limit_bytes=60 * 2**20
        ),
        name="layers_backward",
    )(
        saved_inputs[0, 0].reshape(total, width),
        saved_queries[0, 0],
        norm_gain,
        key_weight[0],
        value_weight[0],
        out_cotangent[0],
        segment_ids[0],
        token_counts,
    )
    results = (gout, dk, dv, gg)
    gout, dk, dv, gg = pl.pallas_call(
        store,
        out_shape=tuple(jax.ShapeDtypeStruct(r.shape, r.dtype) for r in results),
        in_specs=[vmem] * len(results),
        out_specs=(hbm,) * len(results),
        scratch_shapes=[dma((len(results),))],
        compiler_params=pltpu.CompilerParams(vmem_limit_bytes=60 * 2**20),
        name="store_results",
    )(*results)
    return gout[None, None], dk[None], dv[None], gg


def solution(mesh):
    placed = (
        P("section", "dp", None, None, None),
        P("section", "dp", None, None, None),
        P("section", None),
        P("section", None, None),
        P("section", None, None),
        P("dp", None, None, None),
        P("dp", None),
        P("dp", None, None),
    )
    return jax.shard_map(
        functools.partial(shards, mesh.shape["section"], mesh.shape["dp"]),
        mesh=mesh,
        in_specs=placed,
        out_specs=(
            P("section", "dp", None, None, None),
            P("section", "dp", None),
            P("section", "dp", None),
            P("section", None),
        ),
        check_vma=False,
    )
```

```python
import functools

import jax
import jax.numpy as jnp
from jax import lax
from jax.experimental import pallas as pl
from jax.experimental.pallas import tpu as pltpu
from jax.sharding import PartitionSpec as P

HD = 128
KVH = 4
EPS = 1e-05
NY = 4
PARTS = 2
SLICES = 6
Z_GROUPS = 2

f32 = jnp.float32
bf16 = jnp.bfloat16
MESH = pl.DeviceIdType.MESH


def dot(a, b):
    return jnp.dot(a, b, preferred_element_type=f32)


def dot_t(a, b):
    return lax.dot_general(a, b, (((1,), (1,)), ((), ())), preferred_element_type=f32)


def aligned(index, size):
    return pl.ds(pl.multiple_of(index * size, size), size)


def heads(rows, count):
    return jnp.concatenate([rows[:, a * HD : (a + 1) * HD] for a in range(count)], axis=0)


def normalise(x, gain, inv, normed):
    width = x.shape[1]

    def step(r, _):
        rows = aligned(r, 16)
        xb = x[rows, :].astype(f32)
        scale = lax.rsqrt(jnp.sum(xb * xb, axis=1, keepdims=True) * (1.0 / width) + EPS)
        inv[rows, :] = jnp.broadcast_to(scale, (16, 128))
        normed[rows, :] = (xb * scale * gain[...]).astype(bf16)
        return _

    lax.fori_loop(0, x.shape[0] // 16, step, 0)


def project(c, parts, normed, weights, turned, kv32):
    depth = normed.shape[1] // parts
    rows = aligned(c, depth)
    features = normed[:, rows]
    for p, (w, wt) in enumerate(zip(weights, turned)):
        cols = slice(p * w.shape[1], (p + 1) * w.shape[1])
        block = w[rows, :]
        kv32[:, cols] += dot(features, block)
        wt[:, rows] = block.T


def probabilities(m, q, kvb, seg, counts, probs):
    n_rows, width = q.shape[1], q.shape[2]
    per_group = width // HD // KVH
    n = n_rows * per_group
    rows = aligned(m, n_rows)
    seg_row = seg[pl.ds(m, 1), :]
    seg_i = jnp.broadcast_to(jnp.concatenate([seg_row] * per_group, axis=1), (n_rows, n))
    micro = lax.broadcasted_iota(jnp.int32, counts.shape, 1)
    count = jnp.sum(jnp.where(micro == m, counts[...], 0), axis=1, keepdims=True)
    j = lax.broadcasted_iota(jnp.int32, (n_rows, n), 0)
    i = lax.rem(lax.broadcasted_iota(jnp.int32, (n_rows, n), 1), n_rows)
    seg_j = jnp.sum(jnp.where(i == j, seg_i, 0), axis=1, keepdims=True)
    allowed = ((j <= i) & (seg_i * per_group == seg_j) & (j < count)) | (i == j)
    for g in range(KVH):
        keys = kvb[rows, g * HD : (g + 1) * HD]
        queries = heads(q[m, :, g * per_group * HD : (g + 1) * per_group * HD], per_group)
        scores = dot_t(keys, queries) * (HD**-0.5)
        weights = jnp.where(allowed, jnp.exp(scores), 0.0)
        full = weights / jnp.sum(weights, axis=0, keepdims=True)
        probs[m, g] = jnp.where(i < count, full, 0.0)


def attend(m, g, incoming, q, kvb, probs, zgrads, ygrads):
    n_rows, width = q.shape[1], q.shape[2]
    per_group = width // HD // KVH
    kv_cols = KVH * HD
    rows = aligned(m, n_rows)
    values = kvb[rows, kv_cols + g * HD : kv_cols + (g + 1) * HD]
    head_grad = heads(incoming, per_group)
    queries = heads(q[m, :, g * per_group * HD : (g + 1) * per_group * HD], per_group)
    p = probs[m, g]
    prob_grad = dot_t(values, head_grad)
    score_grad = p * (prob_grad - jnp.sum(p * prob_grad, axis=0, keepdims=True)) * (HD**-0.5)
    key_grad = dot(score_grad.astype(bf16), queries).astype(bf16)
    first = (KVH - Z_GROUPS + g) * HD
    ygrads[rows, first : first + HD] = dot(p.astype(bf16), head_grad).astype(bf16)
    if g < Z_GROUPS:
        zgrads[rows, g * HD : (g + 1) * HD] = key_grad
    else:
        ygrads[rows, (g - Z_GROUPS) * HD : (g - Z_GROUPS + 1) * HD] = key_grad


def kernel(
    ns, nz, x_in, q_in, gain_in, kw_in, vw_in, cot, seg_in, counts_in,
    gout, dk_out, dv_out, gg_out, dk, dv, gg,
    x, q, gain, kw, vw, seg, counts, inv, normed, normed_y, all_y, normed_z, all_z, kv32, kvb, probs, kwt, vwt,
    gin, gnext, zgrads, ygrads, gacc, gain_y, gain_zs, gain_zr, pieces, ring_s, ring_r, key_s, key_r,
    x_sem, q_sem, gain_sem, seg_sem, counts_sem, w_sem, cot_sem, next_s, next_r, out_sem, ny_s, ny_r, ny_l, nz_s, nz_r, nz_l, gy2_s, gy2_r, gz2_s, gz2_r, ks_s, ks_r, gy_s, gy_r, gz_s, gz_r, ring_ss, ring_rs, slice_sem, key_sem, gg_sem,
):
    micros, n_rows, width = q.shape
    parts = w_sem.shape[1]
    total = micros * n_rows
    kv_cols = kw.shape[1]
    chunk = width // KVH
    feats = width // (nz * NY)
    sec = lax.axis_index("section")
    dp = lax.axis_index("dp")
    z, y = lax.div(dp, NY), lax.rem(dp, NY)
    is_last = sec == ns - 1
    stages = nz.bit_length() - 1
    half = nz // 2

    def along_z(k):
        return lax.rem(z + k + nz, nz)

    def along_y(k):
        return lax.rem(y + k, NY)

    def flipped(b):
        return z + b - 2 * b * lax.rem(lax.div(z, b), 2)

    def device(zz, yy):
        return (sec, zz * NY + yy)

    y_peers = [device(z, along_y(k)) for k in range(1, NY)]
    up, down = device(along_z(1), y), device(along_z(-1), y)
    z_peers = [device(along_z(k), y) for k in range(1, nz)]
    flips = [device(flipped(1 << i), y) for i in range(stages)]

    def remote(src, dst, ssem, rsem, dev):
        return pltpu.make_async_remote_copy(
            src_ref=src, dst_ref=dst, send_sem=ssem, recv_sem=rsem, device_id=dev, device_id_type=MESH
        )

    def w_copy(p, c):
        rows = aligned(c, width // parts)
        return pltpu.make_async_copy((kw_in, vw_in)[p].at[rows, :], (kw, vw)[p].at[rows, :], w_sem.at[p, c])

    x_copy = pltpu.make_async_copy(x_in, x, x_sem)
    q_copy = pltpu.make_async_copy(q_in, q, q_sem)
    gain_copy = pltpu.make_async_copy(gain_in, gain, gain_sem)
    seg_copy = pltpu.make_async_copy(seg_in, seg, seg_sem)
    counts_copy = pltpu.make_async_copy(counts_in, counts, counts_sem)
    x_copy.start()
    gain_copy.start()
    barrier = pltpu.get_barrier_semaphore()
    above, below = (lax.rem(sec + 1, ns), dp), (lax.rem(sec + ns - 1, ns), dp)
    greeted = y_peers + z_peers + [above, below]
    for peer in greeted:
        pl.semaphore_signal(barrier, inc=1, device_id=peer, device_id_type=MESH)

    for c in range(parts):
        for p in range(2):
            w_copy(p, c).start()

    def cot_copy(g):
        return pltpu.make_async_copy(cot.at[:, :, pl.ds(g * chunk, chunk)], gin.at[1, :, g], cot_sem.at[g])

    kv32[...] = jnp.zeros_like(kv32)
    gacc[...] = jnp.zeros_like(gacc)
    x_copy.wait()
    gain_copy.wait()
    q_copy.start()
    seg_copy.start()
    counts_copy.start()
    normalise(x, gain, inv, normed)

    @pl.when(is_last)
    def _():
        for g in range(KVH):
            cot_copy(g).start()


    def each_part(c, carry):
        for p in range(2):
            w_copy(p, c).wait()
        project(c, parts, normed, (kw, vw), (kwt, vwt), kv32)
        return carry

    lax.fori_loop(0, parts, each_part, 0)
    kvb[...] = kv32[...].astype(bf16)
    q_copy.wait()
    seg_copy.wait()
    counts_copy.wait()

    def each_probs(m, carry):
        probabilities(m, q, kvb, seg, counts, probs)
        return carry

    def turn(b, carry):
        first = b * 128
        owner = lax.div(first, feats)
        oz, oy, offset = lax.div(owner, NY), lax.rem(owner, NY), lax.rem(first, feats)
        block = normed[:, aligned(b, 128)].T
        normed_y[oy, pl.ds(pl.multiple_of(oz * feats + offset, 128), 128), :] = block
        normed_z[oz, pl.ds(pl.multiple_of(oy * feats + offset, 128), 128), :] = block
        return carry

    pl.semaphore_wait(barrier, len(greeted))

    def ny_copy(k):
        return remote(normed_y.at[along_y(k)], all_y.at[:, pl.ds(k * total, total)], ny_s.at[k], ny_r.at[k], y_peers[k - 1])

    def nz_copy(k):
        return remote(normed_z.at[along_z(k)], all_z.at[:, pl.ds(k * total, total)], nz_s.at[k], nz_r.at[k], z_peers[k - 1])

    own_ny = pltpu.make_async_copy(normed_y.at[y], all_y.at[:, pl.ds(0, total)], ny_l)
    own_nz = pltpu.make_async_copy(normed_z.at[z], all_z.at[:, pl.ds(0, total)], nz_l)

    def exchange_normed():
        lax.fori_loop(0, width // 128, turn, 0)
        for k in range(1, NY):
            ny_copy(k).start()
        for k in range(1, nz):
            nz_copy(k).start()
        own_ny.start()
        own_nz.start()

    def next_copy(m, g):
        return remote(gnext.at[m, g], gin.at[0, m, g], next_s.at[m, g], next_r.at[m, g], below)

    def out_copy(g):
        return pltpu.make_async_copy(gnext.at[:, g], gout.at[:, :, pl.ds(g * chunk, chunk)], out_sem.at[g])

    def rows_of(m, k):
        return pl.ds(pl.multiple_of(k * total + m * n_rows, n_rows), n_rows)

    def yg_copy(m, k):
        return remote(ygrads.at[rows_of(m, 0), :], ygrads.at[rows_of(m, k), :], gy2_s.at[k, m], gy2_r.at[k, m], y_peers[k - 1])

    def zg_copy(m, k):
        return remote(zgrads.at[rows_of(m, 0), :], zgrads.at[rows_of(m, k), :], gz2_s.at[k, m], gz2_r.at[k, m], z_peers[k - 1])

    def send_grads(m):
        for k in range(1, NY):
            yg_copy(m, k).start()
        for k in range(1, nz):
            zg_copy(m, k).start()

    def layer(last, m, carry):
        incoming = gin.at[int(last)]
        if last:
            probabilities(m, q, kvb, seg, counts, probs)
        for g in range(KVH):
            if not last:
                next_copy(m, g).wait_recv()
            attend(m, g, incoming[m, g], q, kvb, probs, zgrads, ygrads)
        rows = aligned(m, n_rows)
        pl.when(m == micros - 1)(functools.partial(send_grads, m))
        split = kv_cols - Z_GROUPS * HD
        kg = jnp.concatenate([zgrads[rows, :], ygrads[rows, :split]], axis=1)
        vg = ygrads[rows, split:]
        scale = inv[rows, 0:1]
        along = kg.astype(f32) * kv32[rows, :kv_cols] + vg.astype(f32) * kv32[rows, kv_cols:]
        pulled = jnp.sum(along, axis=1, keepdims=True) * (scale * scale * (1.0 / width))
        for g in range(KVH):
            cols = slice(g * chunk, (g + 1) * chunk)
            grad = (dot(kg, kwt[:, cols]) + dot(vg, vwt[:, cols])) * scale
            xb = x[rows, cols].astype(f32)
            gnext[m, g] = (incoming[m, g].astype(f32) + grad * gain[:, cols] - xb * pulled).astype(bf16)
            next_copy(m, g).start()
            if g == 0:
                pl.when(m < micros - 1)(functools.partial(send_grads, m))
            term = grad * xb
            gacc[:, cols] += term[0:8] + term[8:16] + term[16:24] + term[24:32]
        return carry

    @pl.when(is_last)
    def _():
        for g in range(KVH):
            cot_copy(g).wait()
        lax.fori_loop(0, micros, functools.partial(layer, True), 0)
        exchange_normed()

    @pl.when(jnp.logical_not(is_last))
    def _():
        lax.fori_loop(0, micros, each_probs, 0)
        exchange_normed()
        lax.fori_loop(0, micros, functools.partial(layer, False), 0)

    for g in range(KVH):
        out_copy(g).start()

    part = width // 8
    gsum = jnp.sum(gacc[...], axis=0, keepdims=True)
    for r in range(8):
        gain_y[0, r : r + 1, :] = gsum[:, r * part : (r + 1) * part]

    def gy_copy(k):
        return remote(gain_y.at[0], gain_y.at[k], gy_s.at[k], gy_r.at[k], y_peers[k - 1])

    def gz_copy(i):
        return remote(gain_zs.at[i], gain_zr.at[i], gz_s.at[i], gz_r.at[i], flips[i])

    for k in range(1, NY):
        gy_copy(k).start()

    def gain_stage(i):
        if i == 0:
            for k in range(1, NY):
                gy_copy(k).wait_recv()
            summed = gain_y[0]
            for k in range(1, NY):
                summed = summed + gain_y[k]
        else:
            gz_copy(i - 1).wait_recv()
            summed = gain_zs[i - 1] + gain_zr[i - 1]
        if i < stages:
            gain_zs[i] = summed
            gz_copy(i).start()
        else:
            for r in range(8):
                gg[:, r * part : (r + 1) * part] = summed[r : r + 1, :]

    own_ny.wait()
    for k in range(1, NY):
        ny_copy(k).wait_recv()

    def yg_waits(m, carry):
        for k in range(1, NY):
            yg_copy(m, k).wait_recv()
        return carry

    lax.fori_loop(0, micros, yg_waits, 0)
    slice_cols = ygrads.shape[1] // SLICES

    def each_piece(k, carry):
        pieces[k] = dot(all_y[aligned(along_z(k), feats), :], ygrads[...])
        return carry

    def piece(k, h):
        return pieces[k % nz, :, h * slice_cols : (h + 1) * slice_cols]

    def key_piece(yy):
        return dot(all_z[aligned(yy, feats), :], zgrads[...])

    def key_copy(k):
        return remote(key_s.at[k], key_r.at[k], ks_s.at[k], ks_r.at[k], y_peers[k - 1])

    def zg_waits(m, carry):
        for k in range(1, nz):
            zg_copy(m, k).wait_recv()
        return carry

    def key_send():
        own_nz.wait()
        for k in range(1, nz):
            nz_copy(k).wait_recv()
        lax.fori_loop(0, micros, zg_waits, 0)
        for k in range(1, NY):
            key_s[k] = key_piece(along_y(k)).astype(bf16)
            key_copy(k).start()
        dk[:, : Z_GROUPS * HD] = key_piece(y)

    def ring_copy(way, t, h):
        return remote(
            ring_s.at[way, t, h], ring_r.at[way, t, h], ring_ss.at[way, t, h], ring_rs.at[way, t, h],
            (down, up)[way],
        )

    def in_ring(way, t, h):
        return t > 0 or (t == 0 and h * 2 // SLICES == way)

    each_piece(half, 0)
    for t in range(half):
        for h in range(SLICES):
            for way in range(2):
                if in_ring(way, t, h):
                    value = piece((t - half) if way == 0 else (half - t), h)
                    if in_ring(way, t - 1, h):
                        ring_copy(way, t - 1, h).wait_recv()
                        value = value + ring_r[way, t - 1, h].astype(f32)
                    ring_s[way, t, h] = value.astype(bf16)
                    ring_copy(way, t, h).start()
        if t == 0:
            lax.fori_loop(1, half, each_piece, 0)
            lax.fori_loop(half + 1, nz, each_piece, 0)
            each_piece(0, 0)
            key_send()
        if t <= stages:
            gain_stage(t)
    for t in range(half, stages + 1):
        gain_stage(t)
    def result_copy(h):
        first = Z_GROUPS * HD + h * slice_cols
        cols = pl.ds(first % kv_cols, slice_cols)
        buf, out = ((dk, dk_out), (dv, dv_out))[first // kv_cols]
        return pltpu.make_async_copy(buf.at[:, cols], out.at[:, cols], slice_sem.at[h])

    z_part = pl.ds(0, Z_GROUPS * HD)
    key_out = pltpu.make_async_copy(dk.at[:, z_part], dk_out.at[:, z_part], key_sem)
    gg_copy = pltpu.make_async_copy(gg, gg_out, gg_sem)
    gg_copy.start()
    for k in range(1, NY):
        key_copy(k).wait_recv()
        dk[:, : Z_GROUPS * HD] += key_r[k].astype(f32)
    key_out.start()
    for h in range(SLICES):
        value = piece(0, h)
        for way in range(2):
            ring_copy(way, half - 1, h).wait_recv()
            value = value + ring_r[way, half - 1, h].astype(f32)
        first = Z_GROUPS * HD + h * slice_cols
        out = (dk, dv)[first // kv_cols]
        out[:, first % kv_cols : first % kv_cols + slice_cols] = value
        result_copy(h).start()

    gg_copy.wait()
    key_out.wait()
    for h in range(SLICES):
        result_copy(h).wait()
    def sent(m, carry):
        for g in range(KVH):
            next_copy(m, g).wait_send()
        for k in range(1, NY):
            yg_copy(m, k).wait_send()
        for k in range(1, nz):
            zg_copy(m, k).wait_send()
        return carry

    for g in range(KVH):
        out_copy(g).wait()
    lax.fori_loop(0, micros, sent, 0)
    for k in range(1, NY):
        ny_copy(k).wait_send()
        gy_copy(k).wait_send()
        key_copy(k).wait_send()
    for k in range(1, nz):
        nz_copy(k).wait_send()

    @pl.when(is_last)
    def _():
        for m in range(micros):
            for g in range(KVH):
                next_copy(m, g).wait_recv()

    for i in range(stages):
        gz_copy(i).wait_send()
    for t in range(half):
        for way in range(2):
            for h in range(SLICES):
                if in_ring(way, t, h):
                    ring_copy(way, t, h).wait_send()


def store(gout, dk, dv, gg, gout_to, dk_to, dv_to, gg_to, *held):
    sems = held[-1]
    parts = [(gout.at[m], gout_to.at[m], held[0].at[m]) for m in range(gout.shape[0])]
    parts = [(dk, dk_to, held[1]), (dv, dv_to, held[2]), (gg, gg_to, held[3])] + parts
    loads = [pltpu.make_async_copy(src, buf, sems.at[0, r]) for r, (src, _, buf) in enumerate(parts)]
    stores = [pltpu.make_async_copy(buf, dst, sems.at[1, r]) for r, (_, dst, buf) in enumerate(parts)]
    for copy in loads:
        copy.start()
    for r in range(len(parts)):
        loads[r].wait()
        stores[r].start()
    for copy in stores:
        copy.wait()


def shards(ns, nd, saved_inputs, saved_queries, norm_gain, key_weight, value_weight, out_cotangent, token_counts, segment_ids):
    micros, n_rows, width = saved_inputs.shape[2:]
    kv_cols = key_weight.shape[2]
    total = micros * n_rows
    nz = nd // NY
    per_group = width // HD // KVH
    chunk = width // KVH
    feats = width // nd
    half = nz // 2
    stages = nz.bit_length() - 1
    z_cols = Z_GROUPS * HD
    y_cols = 2 * kv_cols - z_cols
    vmem = pl.BlockSpec(memory_space=pltpu.VMEM)
    hbm = pl.BlockSpec(memory_space=pltpu.HBM)
    dma = pltpu.SemaphoreType.DMA
    gout, dk, dv, gg = pl.pallas_call(
        functools.partial(kernel, ns, nz),
        out_shape=(
            jax.ShapeDtypeStruct((micros, n_rows, width), bf16),
            jax.ShapeDtypeStruct((feats, kv_cols), f32),
            jax.ShapeDtypeStruct((feats, kv_cols), f32),
            jax.ShapeDtypeStruct((1, width), f32),
        ),
        in_specs=[hbm] * 8,
        out_specs=(hbm, hbm, hbm, hbm),
        scratch_shapes=[
            pltpu.VMEM((feats, kv_cols), f32),
            pltpu.VMEM((feats, kv_cols), f32),
            pltpu.VMEM((1, width), f32),
            pltpu.VMEM((total, width), bf16),
            pltpu.VMEM((micros, n_rows, width), bf16),
            pltpu.VMEM((1, width), f32),
            pltpu.VMEM((width, kv_cols), bf16),
            pltpu.VMEM((width, kv_cols), bf16),
            pltpu.VMEM((micros, n_rows), jnp.int32),
            pltpu.VMEM((1, micros), jnp.int32),
            pltpu.VMEM((total, 128), f32),
            pltpu.VMEM((total, width), bf16),
            pltpu.VMEM((NY, nz * feats, total), bf16),
            pltpu.VMEM((nz * feats, NY * total), bf16),
            pltpu.VMEM((nz, NY * feats, total), bf16),
            pltpu.VMEM((NY * feats, nz * total), bf16),
            pltpu.VMEM((total, 2 * kv_cols), f32),
            pltpu.VMEM((total, 2 * kv_cols), bf16),
            pltpu.VMEM((micros, KVH, n_rows, n_rows * per_group), f32),
            pltpu.VMEM((kv_cols, width), bf16),
            pltpu.VMEM((kv_cols, width), bf16),
            pltpu.VMEM((2, micros, KVH, n_rows, chunk), bf16),
            pltpu.VMEM((micros, KVH, n_rows, chunk), bf16),
            pltpu.VMEM((nz * total, z_cols), bf16),
            pltpu.VMEM((NY * total, y_cols), bf16),
            pltpu.VMEM((8, width), f32),
            pltpu.VMEM((NY, 8, width // 8), f32),
            pltpu.VMEM((stages, 8, width // 8), f32),
            pltpu.VMEM((stages, 8, width // 8), f32),
            pltpu.VMEM((nz, feats, y_cols), f32),
            pltpu.VMEM((2, half, SLICES, feats, y_cols // SLICES), bf16),
            pltpu.VMEM((2, half, SLICES, feats, y_cols // SLICES), bf16),
            pltpu.VMEM((NY, feats, z_cols), bf16),
            pltpu.VMEM((NY, feats, z_cols), bf16),
            dma,
            dma,
            dma,
            dma,
            dma,
            dma((2, PARTS)),
            dma((KVH,)),
            dma((micros, KVH)),
            dma((micros, KVH)),
            dma((KVH,)),
            dma((NY,)),
            dma((NY,)),
            dma,
            dma((nz,)),
            dma((nz,)),
            dma,
            dma((NY, micros)),
            dma((NY, micros)),
            dma((nz, micros)),
            dma((nz, micros)),
            dma((NY,)),
            dma((NY,)),
            dma((NY,)),
            dma((NY,)),
            dma((stages,)),
            dma((stages,)),
            dma((2, half, SLICES)),
            dma((2, half, SLICES)),
            dma((SLICES,)),
            dma,
            dma,
        ],
        compiler_params=pltpu.CompilerParams(
            collective_id=0, has_side_effects=True, vmem_limit_bytes=60 * 2**20
        ),
        name="layers_backward",
    )(
        saved_inputs[0, 0].reshape(total, width),
        saved_queries[0, 0],
        norm_gain,
        key_weight[0],
        value_weight[0],
        out_cotangent[0],
        segment_ids[0],
        token_counts,
    )
    results = (gout, dk, dv, gg)
    gout, dk, dv, gg = pl.pallas_call(
        store,
        out_shape=tuple(jax.ShapeDtypeStruct(r.shape, r.dtype) for r in results),
        in_specs=[hbm] * len(results),
        out_specs=(hbm,) * len(results),
        scratch_shapes=[pltpu.VMEM(r.shape, r.dtype) for r in results] + [dma((2, micros + 3))],
        compiler_params=pltpu.CompilerParams(vmem_limit_bytes=60 * 2**20),
        name="store_results",
    )(*results)
    return gout[None, None], dk[None], dv[None], gg


def solution(mesh):
    placed = (
        P("section", "dp", None, None, None),
        P("section", "dp", None, None, None),
        P("section", None),
        P("section", None, None),
        P("section", None, None),
        P("dp", None, None, None),
        P("dp", None),
        P("dp", None, None),
    )
    return jax.shard_map(
        functools.partial(shards, mesh.shape["section"], mesh.shape["dp"]),
        mesh=mesh,
        in_specs=placed,
        out_specs=(
            P("section", "dp", None, None, None),
            P("section", "dp", None),
            P("section", "dp", None),
            P("section", None),
        ),
        check_vma=False,
    )
```

```python
import functools

import jax
import jax.numpy as jnp
from jax import lax
from jax.experimental import pallas as pl
from jax.experimental.pallas import tpu as pltpu
from jax.sharding import PartitionSpec as P

HD = 128
KVH = 4
EPS = 1e-05
NY = 4
PARTS = 2
SLICES = 6
Z_GROUPS = 2

f32 = jnp.float32
bf16 = jnp.bfloat16
MESH = pl.DeviceIdType.MESH


def dot(a, b):
    return jnp.dot(a, b, preferred_element_type=f32)


def dot_t(a, b):
    return lax.dot_general(a, b, (((1,), (1,)), ((), ())), preferred_element_type=f32)


def aligned(index, size):
    return pl.ds(pl.multiple_of(index * size, size), size)


def heads(rows, count):
    return jnp.concatenate([rows[:, a * HD : (a + 1) * HD] for a in range(count)], axis=0)


def normalise(x, gain, inv, normed):
    width = x.shape[1]

    def step(r, _):
        rows = aligned(r, 16)
        xb = x[rows, :].astype(f32)
        scale = lax.rsqrt(jnp.sum(xb * xb, axis=1, keepdims=True) * (1.0 / width) + EPS)
        inv[rows, :] = jnp.broadcast_to(scale, (16, 128))
        normed[rows, :] = (xb * scale * gain[...]).astype(bf16)
        return _

    lax.fori_loop(0, x.shape[0] // 16, step, 0)


def project(c, parts, normed, weights, turned, kv32):
    depth = normed.shape[1] // parts
    rows = aligned(c, depth)
    features = normed[:, rows]
    for p, (w, wt) in enumerate(zip(weights, turned)):
        cols = slice(p * w.shape[1], (p + 1) * w.shape[1])
        block = w[rows, :]
        kv32[:, cols] += dot(features, block)
        wt[:, rows] = block.T


def probabilities(m, q, kvb, seg, counts, probs):
    n_rows, width = q.shape[1], q.shape[2]
    per_group = width // HD // KVH
    n = n_rows * per_group
    rows = aligned(m, n_rows)
    seg_row = seg[pl.ds(m, 1), :]
    seg_i = jnp.broadcast_to(jnp.concatenate([seg_row] * per_group, axis=1), (n_rows, n))
    micro = lax.broadcasted_iota(jnp.int32, counts.shape, 1)
    count = jnp.sum(jnp.where(micro == m, counts[...], 0), axis=1, keepdims=True)
    j = lax.broadcasted_iota(jnp.int32, (n_rows, n), 0)
    i = lax.rem(lax.broadcasted_iota(jnp.int32, (n_rows, n), 1), n_rows)
    seg_j = jnp.sum(jnp.where(i == j, seg_i, 0), axis=1, keepdims=True)
    allowed = ((j <= i) & (seg_i * per_group == seg_j) & (j < count)) | (i == j)
    for g in range(KVH):
        keys = kvb[rows, g * HD : (g + 1) * HD]
        queries = heads(q[m, :, g * per_group * HD : (g + 1) * per_group * HD], per_group)
        scores = dot_t(keys, queries) * (HD**-0.5)
        weights = jnp.where(allowed, jnp.exp(scores), 0.0)
        full = weights / jnp.sum(weights, axis=0, keepdims=True)
        probs[m, g] = jnp.where(i < count, full, 0.0)


def attend(m, g, incoming, q, kvb, probs, zgrads, ygrads):
    n_rows, width = q.shape[1], q.shape[2]
    per_group = width // HD // KVH
    kv_cols = KVH * HD
    rows = aligned(m, n_rows)
    values = kvb[rows, kv_cols + g * HD : kv_cols + (g + 1) * HD]
    head_grad = heads(incoming, per_group)
    queries = heads(q[m, :, g * per_group * HD : (g + 1) * per_group * HD], per_group)
    p = probs[m, g]
    prob_grad = dot_t(values, head_grad)
    score_grad = p * (prob_grad - jnp.sum(p * prob_grad, axis=0, keepdims=True)) * (HD**-0.5)
    key_grad = dot(score_grad.astype(bf16), queries).astype(bf16)
    first = (KVH - Z_GROUPS + g) * HD
    ygrads[rows, first : first + HD] = dot(p.astype(bf16), head_grad).astype(bf16)
    if g < Z_GROUPS:
        zgrads[rows, g * HD : (g + 1) * HD] = key_grad
    else:
        ygrads[rows, (g - Z_GROUPS) * HD : (g - Z_GROUPS + 1) * HD] = key_grad


def kernel(
    ns, nz, x_in, q_in, gain_in, kw_in, vw_in, cot, seg_in, counts_in,
    gout, dk_out, dv_out, gg_out, dk, dv, gg,
    x, q, gain, kw, vw, seg, counts, inv, normed, normed_y, all_y, normed_z, all_z, kv32, kvb, probs, kwt, vwt,
    gin, gnext, zgrads, ygrads, gacc, gain_y, gain_zs, gain_zr, pieces, ring_s, ring_r, key_s, key_r,
    x_sem, q_sem, gain_sem, seg_sem, counts_sem, w_sem, cot_sem, next_s, next_r, out_sem, ny_s, ny_r, ny_l, nz_s, nz_r, nz_l, gy2_s, gy2_r, gz2_s, gz2_r, ks_s, ks_r, gy_s, gy_r, gz_s, gz_r, ring_ss, ring_rs, slice_sem, key_sem, gg_sem,
):
    micros, n_rows, width = q.shape
    parts = w_sem.shape[1]
    total = micros * n_rows
    kv_cols = kw.shape[1]
    chunk = width // KVH
    feats = width // (nz * NY)
    sec = lax.axis_index("section")
    dp = lax.axis_index("dp")
    z, y = lax.div(dp, NY), lax.rem(dp, NY)
    is_last = sec == ns - 1
    stages = nz.bit_length() - 1
    half = nz // 2

    def along_z(k):
        return lax.rem(z + k + nz, nz)

    def along_y(k):
        return lax.rem(y + k, NY)

    def flipped(b):
        return z + b - 2 * b * lax.rem(lax.div(z, b), 2)

    def device(zz, yy):
        return (sec, zz * NY + yy)

    y_peers = [device(z, along_y(k)) for k in range(1, NY)]
    up, down = device(along_z(1), y), device(along_z(-1), y)
    z_peers = [device(along_z(k), y) for k in range(1, nz)]
    flips = [device(flipped(1 << i), y) for i in range(stages)]

    def remote(src, dst, ssem, rsem, dev):
        return pltpu.make_async_remote_copy(
            src_ref=src, dst_ref=dst, send_sem=ssem, recv_sem=rsem, device_id=dev, device_id_type=MESH
        )

    def w_copy(p, c):
        rows = aligned(c, width // parts)
        return pltpu.make_async_copy((kw_in, vw_in)[p].at[rows, :], (kw, vw)[p].at[rows, :], w_sem.at[p, c])

    x_copy = pltpu.make_async_copy(x_in, x, x_sem)
    q_copy = pltpu.make_async_copy(q_in, q, q_sem)
    gain_copy = pltpu.make_async_copy(gain_in, gain, gain_sem)
    seg_copy = pltpu.make_async_copy(seg_in, seg, seg_sem)
    counts_copy = pltpu.make_async_copy(counts_in, counts, counts_sem)
    x_copy.start()
    gain_copy.start()
    barrier = pltpu.get_barrier_semaphore()
    above, below = (lax.rem(sec + 1, ns), dp), (lax.rem(sec + ns - 1, ns), dp)
    greeted = y_peers + z_peers + [above, below]
    for peer in greeted:
        pl.semaphore_signal(barrier, inc=1, device_id=peer, device_id_type=MESH)

    for c in range(parts):
        for p in range(2):
            w_copy(p, c).start()

    def cot_copy(g):
        return pltpu.make_async_copy(cot.at[:, :, pl.ds(g * chunk, chunk)], gin.at[1, :, g], cot_sem.at[g])

    kv32[...] = jnp.zeros_like(kv32)
    gacc[...] = jnp.zeros_like(gacc)
    x_copy.wait()
    gain_copy.wait()
    q_copy.start()
    seg_copy.start()
    counts_copy.start()
    normalise(x, gain, inv, normed)

    @pl.when(is_last)
    def _():
        for g in range(KVH):
            cot_copy(g).start()


    def each_part(c, carry):
        for p in range(2):
            w_copy(p, c).wait()
        project(c, parts, normed, (kw, vw), (kwt, vwt), kv32)
        return carry

    lax.fori_loop(0, parts, each_part, 0)
    kvb[...] = kv32[...].astype(bf16)
    q_copy.wait()
    seg_copy.wait()
    counts_copy.wait()

    def each_probs(m, carry):
        probabilities(m, q, kvb, seg, counts, probs)
        return carry

    def turn(b, carry):
        first = b * 128
        owner = lax.div(first, feats)
        oz, oy, offset = lax.div(owner, NY), lax.rem(owner, NY), lax.rem(first, feats)
        block = normed[:, aligned(b, 128)].T
        normed_y[oy, pl.ds(pl.multiple_of(oz * feats + offset, 128), 128), :] = block
        normed_z[oz, pl.ds(pl.multiple_of(oy * feats + offset, 128), 128), :] = block
        return carry

    pl.semaphore_wait(barrier, len(greeted))

    def ny_copy(k):
        return remote(normed_y.at[along_y(k)], all_y.at[:, pl.ds(k * total, total)], ny_s.at[k], ny_r.at[k], y_peers[k - 1])

    def nz_copy(k):
        return remote(normed_z.at[along_z(k)], all_z.at[:, pl.ds(k * total, total)], nz_s.at[k], nz_r.at[k], z_peers[k - 1])

    own_ny = pltpu.make_async_copy(normed_y.at[y], all_y.at[:, pl.ds(0, total)], ny_l)
    own_nz = pltpu.make_async_copy(normed_z.at[z], all_z.at[:, pl.ds(0, total)], nz_l)

    def exchange_normed():
        lax.fori_loop(0, width // 128, turn, 0)
        for k in range(1, NY):
            ny_copy(k).start()
        for k in range(1, nz):
            nz_copy(k).start()
        own_ny.start()
        own_nz.start()

    def next_copy(m, g):
        return remote(gnext.at[m, g], gin.at[0, m, g], next_s.at[m, g], next_r.at[m, g], below)

    def out_copy(g):
        return pltpu.make_async_copy(gnext.at[:, g], gout.at[:, :, pl.ds(g * chunk, chunk)], out_sem.at[g])

    def rows_of(m, k):
        return pl.ds(pl.multiple_of(k * total + m * n_rows, n_rows), n_rows)

    def yg_copy(m, k):
        return remote(ygrads.at[rows_of(m, 0), :], ygrads.at[rows_of(m, k), :], gy2_s.at[k, m], gy2_r.at[k, m], y_peers[k - 1])

    def zg_copy(m, k):
        return remote(zgrads.at[rows_of(m, 0), :], zgrads.at[rows_of(m, k), :], gz2_s.at[k, m], gz2_r.at[k, m], z_peers[k - 1])

    def send_grads(m):
        for k in range(1, NY):
            yg_copy(m, k).start()
        for k in sorted(range(1, nz), key=lambda k: -min(k, nz - k)):
            zg_copy(m, k).start()

    def layer(last, m, carry):
        incoming = gin.at[int(last)]
        if last:
            probabilities(m, q, kvb, seg, counts, probs)
        for g in range(KVH):
            if not last:
                next_copy(m, g).wait_recv()
            attend(m, g, incoming[m, g], q, kvb, probs, zgrads, ygrads)
        rows = aligned(m, n_rows)
        pl.when(m == micros - 1)(functools.partial(send_grads, m))
        split = kv_cols - Z_GROUPS * HD
        kg = jnp.concatenate([zgrads[rows, :], ygrads[rows, :split]], axis=1)
        vg = ygrads[rows, split:]
        scale = inv[rows, 0:1]
        along = kg.astype(f32) * kv32[rows, :kv_cols] + vg.astype(f32) * kv32[rows, kv_cols:]
        pulled = jnp.sum(along, axis=1, keepdims=True) * (scale * scale * (1.0 / width))
        for g in range(KVH):
            cols = slice(g * chunk, (g + 1) * chunk)
            grad = (dot(kg, kwt[:, cols]) + dot(vg, vwt[:, cols])) * scale
            xb = x[rows, cols].astype(f32)
            gnext[m, g] = (incoming[m, g].astype(f32) + grad * gain[:, cols] - xb * pulled).astype(bf16)
            next_copy(m, g).start()
            if g == 0:
                pl.when(m < micros - 1)(functools.partial(send_grads, m))
            term = grad * xb
            gacc[:, cols] += term[0:8] + term[8:16] + term[16:24] + term[24:32]
        return carry

    @pl.when(is_last)
    def _():
        for g in range(KVH):
            cot_copy(g).wait()
        lax.fori_loop(0, micros, functools.partial(layer, True), 0)
        exchange_normed()

    @pl.when(jnp.logical_not(is_last))
    def _():
        lax.fori_loop(0, micros, each_probs, 0)
        exchange_normed()
        lax.fori_loop(0, micros, functools.partial(layer, False), 0)

    for g in range(KVH):
        out_copy(g).start()

    part = width // 8
    gsum = jnp.sum(gacc[...], axis=0, keepdims=True)
    for r in range(8):
        gain_y[0, r : r + 1, :] = gsum[:, r * part : (r + 1) * part]

    def gy_copy(k):
        return remote(gain_y.at[0], gain_y.at[k], gy_s.at[k], gy_r.at[k], y_peers[k - 1])

    def gz_copy(i):
        return remote(gain_zs.at[i], gain_zr.at[i], gz_s.at[i], gz_r.at[i], flips[i])

    for k in range(1, NY):
        gy_copy(k).start()

    def gain_stage(i):
        if i == 0:
            for k in range(1, NY):
                gy_copy(k).wait_recv()
            summed = gain_y[0]
            for k in range(1, NY):
                summed = summed + gain_y[k]
        else:
            gz_copy(i - 1).wait_recv()
            summed = gain_zs[i - 1] + gain_zr[i - 1]
        if i < stages:
            gain_zs[i] = summed
            gz_copy(i).start()
        else:
            for r in range(8):
                gg[:, r * part : (r + 1) * part] = summed[r : r + 1, :]

    own_ny.wait()
    for k in range(1, NY):
        ny_copy(k).wait_recv()

    def yg_waits(m, carry):
        for k in range(1, NY):
            yg_copy(m, k).wait_recv()
        return carry

    lax.fori_loop(0, micros, yg_waits, 0)
    slice_cols = ygrads.shape[1] // SLICES

    def each_piece(k, carry):
        pieces[k] = dot(all_y[aligned(along_z(k), feats), :], ygrads[...])
        return carry

    def piece(k, h):
        return pieces[k % nz, :, h * slice_cols : (h + 1) * slice_cols]

    def key_piece(yy):
        return dot(all_z[aligned(yy, feats), :], zgrads[...])

    def key_copy(k):
        return remote(key_s.at[k], key_r.at[k], ks_s.at[k], ks_r.at[k], y_peers[k - 1])

    def zg_waits(m, carry):
        for k in range(1, nz):
            zg_copy(m, k).wait_recv()
        return carry

    def key_send():
        own_nz.wait()
        for k in range(1, nz):
            nz_copy(k).wait_recv()
        lax.fori_loop(0, micros, zg_waits, 0)
        for k in range(1, NY):
            key_s[k] = key_piece(along_y(k)).astype(bf16)
            key_copy(k).start()
        dk[:, : Z_GROUPS * HD] = key_piece(y)

    def ring_copy(way, t, h):
        return remote(
            ring_s.at[way, t, h], ring_r.at[way, t, h], ring_ss.at[way, t, h], ring_rs.at[way, t, h],
            (down, up)[way],
        )

    def in_ring(way, t, h):
        return t > 0 or (t == 0 and h * 2 // SLICES == way)

    each_piece(half, 0)
    for t in range(half):
        for h in range(SLICES):
            for way in range(2):
                if in_ring(way, t, h):
                    value = piece((t - half) if way == 0 else (half - t), h)
                    if in_ring(way, t - 1, h):
                        ring_copy(way, t - 1, h).wait_recv()
                        value = value + ring_r[way, t - 1, h].astype(f32)
                    ring_s[way, t, h] = value.astype(bf16)
                    ring_copy(way, t, h).start()
        if t == 0:
            lax.fori_loop(1, half, each_piece, 0)
            lax.fori_loop(half + 1, nz, each_piece, 0)
            each_piece(0, 0)
        if t == min(1, half - 1):
            key_send()
        if t <= stages:
            gain_stage(t)
    for t in range(half, stages + 1):
        gain_stage(t)
    def result_copy(h):
        first = Z_GROUPS * HD + h * slice_cols
        cols = pl.ds(first % kv_cols, slice_cols)
        buf, out = ((dk, dk_out), (dv, dv_out))[first // kv_cols]
        return pltpu.make_async_copy(buf.at[:, cols], out.at[:, cols], slice_sem.at[h])

    z_part = pl.ds(0, Z_GROUPS * HD)
    key_out = pltpu.make_async_copy(dk.at[:, z_part], dk_out.at[:, z_part], key_sem)
    gg_copy = pltpu.make_async_copy(gg, gg_out, gg_sem)
    gg_copy.start()
    for k in range(1, NY):
        key_copy(k).wait_recv()
        dk[:, : Z_GROUPS * HD] += key_r[k].astype(f32)
    key_out.start()
    for h in range(SLICES):
        value = piece(0, h)
        for way in range(2):
            ring_copy(way, half - 1, h).wait_recv()
            value = value + ring_r[way, half - 1, h].astype(f32)
        first = Z_GROUPS * HD + h * slice_cols
        out = (dk, dv)[first // kv_cols]
        out[:, first % kv_cols : first % kv_cols + slice_cols] = value
        result_copy(h).start()

    gg_copy.wait()
    key_out.wait()
    for h in range(SLICES):
        result_copy(h).wait()
    def sent(m, carry):
        for g in range(KVH):
            next_copy(m, g).wait_send()
        for k in range(1, NY):
            yg_copy(m, k).wait_send()
        for k in range(1, nz):
            zg_copy(m, k).wait_send()
        return carry

    for g in range(KVH):
        out_copy(g).wait()
    lax.fori_loop(0, micros, sent, 0)
    for k in range(1, NY):
        ny_copy(k).wait_send()
        gy_copy(k).wait_send()
        key_copy(k).wait_send()
    for k in range(1, nz):
        nz_copy(k).wait_send()

    @pl.when(is_last)
    def _():
        for m in range(micros):
            for g in range(KVH):
                next_copy(m, g).wait_recv()

    for i in range(stages):
        gz_copy(i).wait_send()
    for t in range(half):
        for way in range(2):
            for h in range(SLICES):
                if in_ring(way, t, h):
                    ring_copy(way, t, h).wait_send()


def store(gout, dk, dv, gg, gout_to, dk_to, dv_to, gg_to, *held):
    sems = held[-1]
    parts = [(gout.at[m], gout_to.at[m], held[0].at[m]) for m in range(gout.shape[0])]
    parts = [(dk, dk_to, held[1]), (dv, dv_to, held[2]), (gg, gg_to, held[3])] + parts
    loads = [pltpu.make_async_copy(src, buf, sems.at[0, r]) for r, (src, _, buf) in enumerate(parts)]
    stores = [pltpu.make_async_copy(buf, dst, sems.at[1, r]) for r, (_, dst, buf) in enumerate(parts)]
    for copy in loads:
        copy.start()
    for r in range(len(parts)):
        loads[r].wait()
        stores[r].start()
    for copy in stores:
        copy.wait()


def shards(ns, nd, saved_inputs, saved_queries, norm_gain, key_weight, value_weight, out_cotangent, token_counts, segment_ids):
    micros, n_rows, width = saved_inputs.shape[2:]
    kv_cols = key_weight.shape[2]
    total = micros * n_rows
    nz = nd // NY
    per_group = width // HD // KVH
    chunk = width // KVH
    feats = width // nd
    half = nz // 2
    stages = nz.bit_length() - 1
    z_cols = Z_GROUPS * HD
    y_cols = 2 * kv_cols - z_cols
    vmem = pl.BlockSpec(memory_space=pltpu.VMEM)
    hbm = pl.BlockSpec(memory_space=pltpu.HBM)
    dma = pltpu.SemaphoreType.DMA
    gout, dk, dv, gg = pl.pallas_call(
        functools.partial(kernel, ns, nz),
        out_shape=(
            jax.ShapeDtypeStruct((micros, n_rows, width), bf16),
            jax.ShapeDtypeStruct((feats, kv_cols), f32),
            jax.ShapeDtypeStruct((feats, kv_cols), f32),
            jax.ShapeDtypeStruct((1, width), f32),
        ),
        in_specs=[hbm] * 8,
        out_specs=(hbm, hbm, hbm, hbm),
        scratch_shapes=[
            pltpu.VMEM((feats, kv_cols), f32),
            pltpu.VMEM((feats, kv_cols), f32),
            pltpu.VMEM((1, width), f32),
            pltpu.VMEM((total, width), bf16),
            pltpu.VMEM((micros, n_rows, width), bf16),
            pltpu.VMEM((1, width), f32),
            pltpu.VMEM((width, kv_cols), bf16),
            pltpu.VMEM((width, kv_cols), bf16),
            pltpu.VMEM((micros, n_rows), jnp.int32),
            pltpu.VMEM((1, micros), jnp.int32),
            pltpu.VMEM((total, 128), f32),
            pltpu.VMEM((total, width), bf16),
            pltpu.VMEM((NY, nz * feats, total), bf16),
            pltpu.VMEM((nz * feats, NY * total), bf16),
            pltpu.VMEM((nz, NY * feats, total), bf16),
            pltpu.VMEM((NY * feats, nz * total), bf16),
            pltpu.VMEM((total, 2 * kv_cols), f32),
            pltpu.VMEM((total, 2 * kv_cols), bf16),
            pltpu.VMEM((micros, KVH, n_rows, n_rows * per_group), f32),
            pltpu.VMEM((kv_cols, width), bf16),
            pltpu.VMEM((kv_cols, width), bf16),
            pltpu.VMEM((2, micros, KVH, n_rows, chunk), bf16),
            pltpu.VMEM((micros, KVH, n_rows, chunk), bf16),
            pltpu.VMEM((nz * total, z_cols), bf16),
            pltpu.VMEM((NY * total, y_cols), bf16),
            pltpu.VMEM((8, width), f32),
            pltpu.VMEM((NY, 8, width // 8), f32),
            pltpu.VMEM((stages, 8, width // 8), f32),
            pltpu.VMEM((stages, 8, width // 8), f32),
            pltpu.VMEM((nz, feats, y_cols), f32),
            pltpu.VMEM((2, half, SLICES, feats, y_cols // SLICES), bf16),
            pltpu.VMEM((2, half, SLICES, feats, y_cols // SLICES), bf16),
            pltpu.VMEM((NY, feats, z_cols), bf16),
            pltpu.VMEM((NY, feats, z_cols), bf16),
            dma,
            dma,
            dma,
            dma,
            dma,
            dma((2, PARTS)),
            dma((KVH,)),
            dma((micros, KVH)),
            dma((micros, KVH)),
            dma((KVH,)),
            dma((NY,)),
            dma((NY,)),
            dma,
            dma((nz,)),
            dma((nz,)),
            dma,
            dma((NY, micros)),
            dma((NY, micros)),
            dma((nz, micros)),
            dma((nz, micros)),
            dma((NY,)),
            dma((NY,)),
            dma((NY,)),
            dma((NY,)),
            dma((stages,)),
            dma((stages,)),
            dma((2, half, SLICES)),
            dma((2, half, SLICES)),
            dma((SLICES,)),
            dma,
            dma,
        ],
        compiler_params=pltpu.CompilerParams(
            collective_id=0, has_side_effects=True, vmem_limit_bytes=60 * 2**20
        ),
        name="layers_backward",
    )(
        saved_inputs[0, 0].reshape(total, width),
        saved_queries[0, 0],
        norm_gain,
        key_weight[0],
        value_weight[0],
        out_cotangent[0],
        segment_ids[0],
        token_counts,
    )
    results = (gout, dk, dv, gg)
    gout, dk, dv, gg = pl.pallas_call(
        store,
        out_shape=tuple(jax.ShapeDtypeStruct(r.shape, r.dtype) for r in results),
        in_specs=[hbm] * len(results),
        out_specs=(hbm,) * len(results),
        scratch_shapes=[pltpu.VMEM(r.shape, r.dtype) for r in results] + [dma((2, micros + 3))],
        compiler_params=pltpu.CompilerParams(vmem_limit_bytes=60 * 2**20),
        name="store_results",
    )(*results)
    return gout[None, None], dk[None], dv[None], gg


def solution(mesh):
    placed = (
        P("section", "dp", None, None, None),
        P("section", "dp", None, None, None),
        P("section", None),
        P("section", None, None),
        P("section", None, None),
        P("dp", None, None, None),
        P("dp", None),
        P("dp", None, None),
    )
    return jax.shard_map(
        functools.partial(shards, mesh.shape["section"], mesh.shape["dp"]),
        mesh=mesh,
        in_specs=placed,
        out_specs=(
            P("section", "dp", None, None, None),
            P("section", "dp", None),
            P("section", "dp", None),
            P("section", None),
        ),
        check_vma=False,
    )
```
